512 devices in a mesh: bond: 16 (over x, y_lo, core), site: 32 (over y_hi, z).
Axes of the slice: x: 4, y: 8 (y_hi: 4, y_lo: 2; y = y_hi * 2 + y_lo), z: 8, core: 2. Of those that a mesh axis runs over, the one named last changes fastest.
Arguments:
- two_site: float32 [32, 4096, 2048], P('site', None, 'bond')
- keep_list: int32 [32, 1024], P('site', 'bond'), may hold values from 0 to 127, as said below
- owner_map: int32 [32, 1024, 1], P('site', 'bond'), may hold values from 0 to 31; in each aligned block of 64 rows (0 to 63, 64 to 127, ..., all dimensions but the last counted through in order) at most 4 rows name the same one
Outputs:
- arrivals: float32 [32, 16, 32, 4, 4096], P('site', 'bond')
The draws below stay inside these ranges and needn't reach their ends.
Inputs may be any that keep to these rules, and one draw needn't show every extreme that they name: `keep_list`: the 64 entries of one block are distinct column numbers of that block. `owner_map`: among the 64 kept columns of one block at most 4 go to one owner, and some owner gets exactly 4.
All inputs are finite; a program needn't handle non-finite values.
Results may differ from the reference program's by a relative error of at most 0.00011.
Values sent between devices are 32-bit elements; how exact they have to be, the bound alone decides.
No kernel may reach another device: no remote copies, remote signals or barrier semaphores. Data moves between devices by JAX's collectives and lax.ppermute only.
A program may use at most 64 MiB of HBM per device.

```python
import math
import jax
import jax.numpy as jnp
import numpy as np
from jax import lax

ROWS = 4096
BLK = 128
KEEP = 64
CAP = 4
NS_STEPS = 5
BLOCKS = 16
COLS = 2048
SITES = 32
N_SITE = 32


def draw_two_site(key, part):
    key = jax.random.fold_in(key, 7)
    key_base, key_cols, key_rows = jax.random.split(key, 3)
    shape = (SITES, ROWS, COLS)
    position = (jnp.arange(COLS) // BLK).astype(jnp.float32)
    rise = 3.0 ** (position / (COLS // BLK - 1))
    col_scale = jnp.exp(jax.random.uniform(key_cols, (SITES, 1, COLS)) * jnp.log(10.0)) * rise[None, None, :]
    row_scale = jnp.exp(jax.random.uniform(key_rows, (SITES, ROWS, 1)) * jnp.log(10.0))
    values = jax.random.normal(key_base, shape)
    return (values * row_scale * col_scale).astype(jnp.float32)


def draw_keep_list(key, part):
    key = jax.random.fold_in(key, 11)
    scores = jax.random.randint(key, (SITES * BLOCKS, BLK), 0, 2 ** 20) * BLK + jnp.arange(BLK)[None, :]
    chosen = jnp.argsort(scores, axis=1, stable=True)[:, :KEEP]
    return chosen.reshape(SITES, BLOCKS * KEEP).astype(jnp.int32)


def assign_block(stream_key, own, number, rows, amount, top, limit, skew):
    ranking = jax.random.permutation(stream_key, amount)
    packed, ordinary = load_shares(amount, rows * top, limit, skew, True), load_shares(amount, rows * top, limit, skew, False)
    places = jnp.arange(amount)

    def named(lengths, offset_by):
        used = int((lengths > 0).sum())
        fixed = max(1, used // 4)
        moved = fixed + (places - fixed + offset_by * (used - fixed)) % max(1, amount - fixed)
        return jnp.zeros((amount,), jnp.int32).at[ranking[jnp.where(places < fixed, places, moved)]].set(jnp.asarray(lengths, jnp.int32))

    lengths = jnp.where(number % 4 == 0, named(packed, number // 4), named(ordinary, number - number // 4 - 1))
    mixed = jax.random.permutation(jax.random.fold_in(own, 3), amount)
    giver, receiver = mixed[0:amount // 2 * 2:2], mixed[1:amount // 2 * 2:2]
    margin = jnp.minimum(lengths[giver] - 1, limit - lengths[receiver]) // 2
    margin = jnp.where((giver == ranking[0]) | (receiver == ranking[0]) | (lengths[receiver] == 0), 0, jnp.maximum(margin, 0))
    moved = jax.random.randint(jax.random.fold_in(own, 4), (amount // 2,), 0, 1 << 20) % (margin + 1)
    lengths = lengths.at[giver].add(-moved).at[receiver].add(moved)
    members = jnp.searchsorted(jnp.cumsum(lengths), jnp.arange(rows * top), side="right").astype(jnp.int32)
    grid = members.reshape(top, rows).T
    grid = grid[jax.random.permutation(jax.random.fold_in(own, 1), rows)]
    offset_by = jax.random.randint(jax.random.fold_in(own, 2), (rows, 1), 0, top)
    return jnp.take_along_axis(grid, (jnp.arange(top)[None, :] + offset_by) % top, axis=1)


def load_shares(amount, total, bound, skew, full):
    weights = [(1 << 20) // math.isqrt(rank ** skew) + 1 for rank in range(1, amount + 1)]
    largest = bound if full else min(bound, max(-(-total // amount), total * weights[0] // sum(weights)))
    least = 1 if total - largest >= amount - 1 else 0
    holding, spare = [largest] + [least] * (amount - 1), total - largest - least * (amount - 1)
    while spare > 0:
        movable = [i for i in range(1, amount) if holding[i] < largest] or [i for i in range(1, amount) if holding[i] < bound]
        whole, remaining = sum([weights[i] for i in movable]), spare
        for i in movable:
            extra = min(bound - holding[i], max(1, remaining * weights[i] // whole), spare)
            holding[i] = holding[i] + extra
            spare = spare - extra
    return np.array(holding)


def setup_inputs(seed: int = 0) -> dict:
    splits = jax.random.split(jax.random.key(seed), 4)
    two_site = draw_two_site(jax.random.fold_in(splits[3], 71), 0)
    keep_list = draw_keep_list(jax.random.fold_in(splits[3], 71), 0)
    owner_map_keys = jax.random.split(jax.random.fold_in(splits[2], 1), SITES * (BLOCKS * KEEP) // KEEP)
    owner_map_turns = jax.random.permutation(jax.random.fold_in(splits[2], 3), SITES * (BLOCKS * KEEP) // KEEP)
    owner_map = jax.vmap(lambda own, number: assign_block(jax.random.fold_in(splits[2], 2), own, number, KEEP, N_SITE, 1, CAP, 2))(owner_map_keys, owner_map_turns).reshape((SITES, BLOCKS * KEEP, 1))
    return dict(two_site=two_site, keep_list=keep_list, owner_map=owner_map)


HIGH = lax.Precision.HIGHEST

def rotation(gram):
    width = gram.shape[0]
    inverse = 1.0 / jnp.sqrt(jnp.diagonal(gram))
    correlation = gram * inverse[:, None] * inverse[None, :]
    upper_part = jnp.triu(correlation, 1)
    skew_part = 0.5 * (upper_part - upper_part.T)
    identity = jnp.eye(width, dtype=jnp.float32)
    iterate = (identity + skew_part) / jnp.sqrt(1.0 + jnp.sum(skew_part * skew_part))
    for sweep_step in range(NS_STEPS):
        square = jnp.dot(iterate.T, iterate, precision=HIGH, preferred_element_type=jnp.float32)
        iterate = 0.5 * jnp.dot(iterate, 3.0 * identity - square, precision=HIGH, preferred_element_type=jnp.float32)
    return iterate

def rotate_pair(pair_block):
    gram = jnp.einsum('rc,rd->cd', pair_block, pair_block, precision=HIGH, preferred_element_type=jnp.float32)
    return jnp.dot(pair_block, rotation(gram), precision=HIGH, preferred_element_type=jnp.float32)

def reference(two_site, keep_list, owner_map):
    blocks = two_site.reshape(SITES, ROWS, BLOCKS, BLK).transpose(0, 2, 1, 3)
    levels = BLOCKS.bit_length() - 1
    for bit_place in [levels - 1, 0]:
        lows = np.array([number for number in range(BLOCKS) if number >> bit_place & 1 == 0])
        highs = lows + (1 << bit_place)
        pairs = jnp.concatenate([blocks[:, lows], blocks[:, highs]], axis=-1)
        pairs = pairs.reshape(SITES * (BLOCKS // 2), ROWS, 2 * BLK)
        rotated = lax.map(rotate_pair, pairs).reshape(SITES, BLOCKS // 2, ROWS, 2 * BLK)
        blocks = blocks.at[:, lows].set(rotated[..., :BLK]).at[:, highs].set(rotated[..., BLK:])
    keep_index = keep_list.reshape(SITES, BLOCKS, 1, KEEP).astype(jnp.int32)
    kept_cols = jnp.take_along_axis(blocks, keep_index, axis=3).transpose(0, 1, 3, 2)
    norms = lax.optimization_barrier(jnp.sum(kept_cols * kept_cols, axis=(1, 2, 3)))
    scaled = kept_cols * jnp.sqrt(ROWS * BLOCKS * KEEP / norms)[:, None, None, None]
    owners = owner_map.reshape(SITES, BLOCKS, KEEP).astype(jnp.int32)
    order = jnp.arange(KEEP, dtype=jnp.int32)
    before = order[None, :] < order[:, None]
    same = owners[..., :, None] == owners[..., None, :]
    slots = lax.optimization_barrier(jnp.sum((same & before).astype(jnp.int32), axis=-1)).astype(jnp.int32)
    source = jnp.broadcast_to(jnp.arange(SITES, dtype=jnp.int32)[:, None, None], owners.shape)
    column_block = jnp.broadcast_to(jnp.arange(BLOCKS, dtype=jnp.int32)[None, :, None], owners.shape)
    arrivals = jnp.zeros((SITES, BLOCKS, SITES, CAP, ROWS), jnp.float32)
    arrivals = arrivals.at[owners, column_block, source, slots].set(scaled)
    return arrivals
```

```python
import jax
import jax.numpy as jnp
from jax import lax
from jax.experimental import pallas as pl
from jax.experimental.pallas import tpu as pltpu
from jax.sharding import PartitionSpec as P

NS_STEPS = 5
LANES = 128
F32 = jnp.float32
BF16 = jnp.bfloat16

NN = ((1,), (0,))
NT = ((1,), (1,))
TN = ((0,), (0,))


def split(value):
    high = value.astype(BF16)
    return high, (value - high.astype(F32)).astype(BF16)


def dot(left, right, contract):
    return lax.dot_general(left, right, (contract, ((), ())), preferred_element_type=F32)


def product(left, right, contract):
    return dot(left[0], right[0], contract) + (
        dot(left[0], right[1], contract) + dot(left[1], right[0], contract)
    )


def gram_kernel(own_ref, next_ref, top_ref, bottom_ref):
    half = own_ref.shape[1]
    pair = split(jnp.concatenate([own_ref[...], next_ref[...]], 1))
    gram = product(pair, pair, TN)

    @pl.when(pl.program_id(0) == 0)
    def _():
        top_ref[...] = gram[:half]
        bottom_ref[...] = gram[half:]

    @pl.when(pl.program_id(0) > 0)
    def _():
        top_ref[...] += gram[:half]
        bottom_ref[...] += gram[half:]


def pair_gram(own, neighbour, steps):
    rows, width = own.shape
    tile = rows // steps
    shape = jax.ShapeDtypeStruct((width, 2 * width), F32)
    rows_in = pl.BlockSpec((tile, width), lambda i: (i, 0))
    whole = pl.BlockSpec((width, 2 * width), lambda i: (0, 0))
    return pl.pallas_call(
        gram_kernel,
        grid=(steps,),
        in_specs=[rows_in, rows_in],
        out_specs=[whole, whole],
        out_shape=[shape, shape],
        name="pair_gram",
    )(own, neighbour)


def cross_kernel(place_ref, own_ref, next_ref, far_ref, next_far_ref, before_ref, out_ref):
    here = split(jnp.concatenate([own_ref[...], next_ref[...]], 1))
    there = split(jnp.concatenate([far_ref[...], next_far_ref[...]], 1))
    gram = product(here, there, TN)

    @pl.when(pl.program_id(0) == 0)
    def _():
        out_ref[...] = before_ref[...] + gram

    @pl.when(pl.program_id(0) > 0)
    def _():
        out_ref[...] += gram


def cross_gram(place, own, neighbour, far, next_far, before, start, steps):
    rows, width = far.shape
    tile = rows // steps
    half = own.shape[0] // 2
    first = start // tile
    mine = pl.BlockSpec((tile, width), lambda i, place: (place[0] * (half // tile) + first + i, 0))
    rows_in = pl.BlockSpec((tile, width), lambda i, place: (i, 0))
    whole = pl.BlockSpec((2 * width, 2 * width), lambda i, place: (0, 0))
    return pl.pallas_call(
        cross_kernel,
        grid_spec=pltpu.PrefetchScalarGridSpec(
            num_scalar_prefetch=1,
            grid=(steps,),
            in_specs=[mine, mine, rows_in, rows_in, whole],
            out_specs=whole,
        ),
        out_shape=jax.ShapeDtypeStruct((2 * width, 2 * width), F32),
        name="cross_gram",
    )(place, own, neighbour, far, next_far, before)


def rotations(grams, sign):
    width = grams[0].shape[0]
    half = width // 2
    row = lax.broadcasted_iota(jnp.int32, (width, width), 0)
    column = lax.broadcasted_iota(jnp.int32, (width, width), 1)
    diagonal = (row == column).astype(F32)
    order = jnp.where(row < column, 0.5, -0.5) * (1.0 - diagonal)
    order = jnp.where((row < half) == (column < half), order, order * sign)
    iterates = []
    for gram in grams:
        inverse_row = 1.0 / jnp.sqrt(jnp.sum(gram * diagonal, axis=0, keepdims=True))
        inverse_column = 1.0 / jnp.sqrt(jnp.sum(gram * diagonal, axis=1, keepdims=True))
        skew = gram * inverse_column * inverse_row * order
        iterates.append((diagonal + skew) / jnp.sqrt(1.0 + jnp.sum(skew * skew)))
    for step in range(NS_STEPS):
        parts = [split(iterate) for iterate in iterates]
        squares = [product(part, part, NT) for part in parts]
        rests = [0.5 * (diagonal - square) for square in squares]
        iterates = [
            iterate + product(part, split(rest), NN)
            for iterate, part, rest in zip(iterates, parts, rests)
        ]
    return iterates


def symmetric(first, cross, second):
    return jnp.concatenate(
        [jnp.concatenate([first, cross], 1), jnp.concatenate([cross.T, second], 1)], 0
    )


def turn_kernel(
    place_ref, top_ref, bottom_ref, far_top_ref, far_bottom_ref, cross_ref, far_cross_ref, route_ref, kept_ref,
    block_ref, next_ref, far_a_ref, far_b_ref, next_far_a_ref, next_far_b_ref,
    out_ref, norm_ref, rows_ref, sems,
):
    rows, width = rows_ref.shape[1:]
    part = rows // 2
    upper, right = place_ref[0], place_ref[1]
    start = pl.multiple_of(upper * rows, rows)
    copies = [
        pltpu.make_async_copy(source, target, sems.at[number])
        for number, (source, target) in enumerate(
            [
                (block_ref.at[pl.ds(start, rows)], rows_ref.at[0]),
                (next_ref.at[pl.ds(start, rows)], rows_ref.at[2]),
                (far_a_ref, rows_ref.at[1, :part]),
                (far_b_ref, rows_ref.at[1, part:]),
                (next_far_a_ref, rows_ref.at[3, :part]),
                (next_far_b_ref, rows_ref.at[3, part:]),
            ]
        )
    ]
    for copy in copies:
        copy.start()
    sign_far = jnp.where(upper == 0, 1.0, -1.0)
    sign_next = jnp.where(right == 0, 1.0, -1.0)

    cross = cross_ref[...] + far_cross_ref[...].T
    top, bottom, far_top, far_bottom = top_ref[...], bottom_ref[...], far_top_ref[...], far_bottom_ref[...]
    lo, hi = slice(0, width), slice(width, 2 * width)
    gram_01 = symmetric(top[:, lo], cross[lo, lo], far_top[:, lo])
    gram_23 = symmetric(bottom[:, hi], cross[hi, hi], far_bottom[:, lo])
    mixed = jnp.concatenate(
        [
            jnp.concatenate([top[:, hi], cross[lo, hi]], 1),
            jnp.concatenate([cross[hi, lo].T, far_top[:, hi]], 1),
        ],
        0,
    )
    turn_01, turn_23 = rotations([gram_01, gram_23], sign_far)
    s_01, s_23 = split(turn_01), split(turn_23)
    s_01t, s_23t = split(turn_01.T), split(turn_23.T)
    half_01 = split(product(split(gram_01), s_01, NN))
    half_23 = split(product(split(gram_23), s_23, NN))
    half_mixed = split(product(split(mixed), s_23, NN))

    def corner(left, right, which):
        return product(
            (left[0][which], left[1][which]), (right[0][:, which], right[1][:, which]), NN
        )

    grams = [
        symmetric(corner(s_01t, half_01, w), corner(s_01t, half_mixed, w), corner(s_23t, half_23, w))
        for w in (lo, hi)
    ]
    seconds = rotations(grams, sign_next)

    total = jnp.zeros((1, 1), F32)
    routed = [0.0, 0.0]
    for number, (gram, second, which) in enumerate(zip(grams, seconds, (lo, hi))):
        parts = split(second)
        moved = product(split(gram), parts, NN) * second
        kept = jnp.concatenate([kept_ref[number : number + 1], kept_ref[number + 2 : number + 3]], 1)
        total += jnp.sum(jnp.sum(moved, axis=0, keepdims=True) * kept, axis=1, keepdims=True)
        turned = jnp.concatenate(
            [
                product([p[:, which] for p in s_01], [p[lo, lo] for p in parts], NN),
                product([p[:, which] for p in s_23], [p[hi, lo] for p in parts], NN),
            ],
            0,
        )
        route = route_ref[number].astype(BF16)
        routed = [into + dot(piece, route, NN) for into, piece in zip(routed, split(turned))]
    norm_ref[...] = jnp.broadcast_to(total, norm_ref.shape)

    placed = [piece.T.astype(BF16) for piece in routed]
    left = [piece[:, : 2 * width] for piece in placed]
    right_side = [piece[:, 2 * width :] for piece in placed]
    for copy in copies:
        copy.wait()
    chunk = min(512, rows)
    for begin in range(0, rows, chunk):
        span = slice(begin, begin + chunk)
        near = split(jnp.concatenate([rows_ref[0, span], rows_ref[1, span]], 1))
        far = split(jnp.concatenate([rows_ref[2, span], rows_ref[3, span]], 1))
        out_ref[:, span] = product(left, near, NT) + product(right_side, far, NT)


def turn(place, grams, routes, kept, blocks):
    rows, width = blocks[0].shape
    rows = rows // 2
    vmem = pl.BlockSpec(memory_space=pltpu.VMEM)
    anywhere = pl.BlockSpec(memory_space=pl.ANY)
    return pl.pallas_call(
        turn_kernel,
        in_specs=[pl.BlockSpec(memory_space=pltpu.SMEM)] + [vmem] * 8 + [anywhere] * 6,
        out_specs=[vmem, vmem],
        out_shape=[
            jax.ShapeDtypeStruct((2 * width, rows), F32),
            jax.ShapeDtypeStruct((8, width), F32),
        ],
        scratch_shapes=[pltpu.VMEM((4, rows, width), F32), pltpu.SemaphoreType.DMA((6,))],
        compiler_params=pltpu.CompilerParams(vmem_limit_bytes=40 * 1024 * 1024),
        name="turn",
    )(place, *grams, routes, kept, *blocks)


def from_partner(value, axis, distance):
    pairs = [(source, source ^ distance) for source in range(lax.axis_size(axis))]
    return lax.ppermute(value, axis, pairs)


def route_of(listed, side, groups, width):
    keep, owners = listed[0], listed[1]
    kept = keep.shape[0]
    order = jnp.arange(kept, dtype=jnp.int32)
    same = owners[:, None] == owners[None, :]
    slot = jnp.sum((same & (order[None, :] < order[:, None])).astype(jnp.int32), axis=1)
    capacity = max(2, 2 * kept // groups)
    target = (owners * 2 + side) * capacity + slot
    places = jnp.arange(2 * groups * capacity, dtype=jnp.int32)
    columns = jnp.arange(width, dtype=jnp.int32)
    picked = (keep[:, None] == columns[None, :]).astype(BF16)
    placed = (target[:, None] == places[None, :]).astype(BF16)
    return lax.dot_general(picked, placed, (TN, ((), ())), preferred_element_type=F32)


def on_device(two_site, keep_list, owner_map):
    block = two_site[0]
    rows, width = block.shape
    half, quarter = rows // 2, rows // 4
    count, groups = lax.axis_size("bond"), lax.axis_size("site")
    far = count // 2
    position = lax.axis_index("bond")
    upper = position // far
    place = jnp.stack([upper, position & 1]).astype(jnp.int32)

    start = (1 - upper) * half
    far_a = from_partner(lax.dynamic_slice_in_dim(block, start, quarter), "bond", far)
    far_b = from_partner(lax.dynamic_slice_in_dim(block, start + quarter, quarter), "bond", far)
    neighbour = from_partner(block, "bond", 1)
    listed = jnp.stack([keep_list[0], owner_map[0, :, 0]])
    listed = jnp.concatenate([listed, from_partner(listed, "bond", far)])
    routes = jnp.stack(
        [
            route_of(listed[:2], upper, groups, width),
            route_of(listed[2:], 1 - upper, groups, width),
        ]
    )
    lists = jnp.concatenate([listed[::2], from_partner(listed[::2], "bond", 1)])
    columns = jnp.arange(width, dtype=jnp.int32)
    kept = jnp.sum((lists[:, :, None] == columns).astype(F32), axis=1)

    top, bottom = pair_gram(block, neighbour, 4)
    far_top = from_partner(top, "bond", far)
    next_far_a = from_partner(far_a, "bond", 1)
    far_bottom = from_partner(far_top, "bond", 1)
    next_far_b = from_partner(far_b, "bond", 1)
    cross = jnp.zeros((2 * width, 2 * width), F32)
    cross = cross_gram(place, block, neighbour, far_a, next_far_a, cross, 0, 2)
    cross = cross_gram(place, block, neighbour, far_b, next_far_b, cross, quarter, 2)
    far_cross = from_partner(cross, "bond", far)

    outgoing, squares = turn(
        place,
        (top, bottom, far_top, far_bottom, cross, far_cross),
        routes,
        kept,
        (block, neighbour, far_a, far_b, next_far_a, next_far_b),
    )
    for distance in [1 << bit for bit in range(1, far.bit_length() - 1)]:
        squares = squares + from_partner(squares, "bond", distance)
    keep_count = keep_list.shape[1]
    scale = jnp.sqrt(rows * count * keep_count / squares[0, 0])
    capacity = max(2, 2 * keep_count // groups)
    members = [
        [(first + far * side) * groups + site for site in range(groups) for side in range(2)]
        for first in range(far)
    ]
    outgoing = (outgoing * scale).reshape(2 * groups, capacity, half // LANES, LANES)
    arrived = lax.all_to_all(
        outgoing.transpose(0, 2, 1, 3),
        ("bond", "site"),
        split_axis=0,
        concat_axis=0,
        tiled=True,
        axis_index_groups=members,
    )
    arrived = arrived.reshape(groups, rows // LANES, capacity, LANES).transpose(0, 2, 1, 3)
    return arrived.reshape(1, 1, groups, capacity, rows)


def solution(mesh):
    return jax.shard_map(
        on_device,
        mesh=mesh,
        in_specs=(P("site", None, "bond"), P("site", "bond"), P("site", "bond", None)),
        out_specs=P("site", "bond", None, None, None),
        check_vma=False,
    )
```

```python
import functools

import jax
import jax.numpy as jnp
from jax import lax
from jax.experimental import pallas as pl
from jax.experimental.pallas import tpu as pltpu
from jax.sharding import PartitionSpec as P

NS_STEPS = 5
LANES = 128
F32 = jnp.float32
BF16 = jnp.bfloat16

NN = ((1,), (0,))
NT = ((1,), (1,))
TN = ((0,), (0,))


def piece_sizes(rows):
    return (rows // 2, rows // 2)


def split(value):
    high = value.astype(BF16)
    return high, (value - high.astype(F32)).astype(BF16)


def dot(left, right, contract):
    return lax.dot_general(left, right, (contract, ((), ())), preferred_element_type=F32)


def product(left, right, contract):
    return dot(left[0], right[0], contract) + (
        dot(left[0], right[1], contract) + dot(left[1], right[0], contract)
    )


VMEM = pl.BlockSpec(memory_space=pltpu.VMEM)
SMEM = pl.BlockSpec(memory_space=pltpu.SMEM)
ANY = pl.BlockSpec(memory_space=pl.ANY)


def array(*shape):
    return jax.ShapeDtypeStruct(shape, F32)


BRIEF = pl.CostEstimate(flops=1, bytes_accessed=1, transcendentals=0)


def params(mebibytes):
    return pltpu.CompilerParams(vmem_limit_bytes=mebibytes * 1024 * 1024)


def after_kernel(first_ref, value_ref, out_ref):
    out_ref[...] = value_ref[...]


def after(first, value):
    return pl.pallas_call(
        after_kernel,
        in_specs=[ANY, VMEM],
        out_specs=VMEM,
        out_shape=jax.ShapeDtypeStruct(value.shape, value.dtype),
        compiler_params=params(8),
        cost_estimate=BRIEF,
        name="after",
    )(first, value)


def gram_kernel(own_ref, next_ref, top_ref, bottom_ref):
    rows, half = own_ref.shape
    chunk = min(1024, rows)
    high = low = jnp.zeros((2 * half, 2 * half), F32)
    for begin in range(0, rows, chunk):
        span = slice(begin, begin + chunk)
        pair = split(jnp.concatenate([own_ref[span], next_ref[span]], 1))
        high += dot(pair[0], pair[0], TN)
        low += dot(pair[0], pair[1], TN)
    gram = high + (low + low.T)
    top_ref[...] = gram[:half]
    bottom_ref[...] = gram[half:]


def pair_gram(own, neighbour):
    width = own.shape[1]
    return pl.pallas_call(
        gram_kernel,
        in_specs=[VMEM, VMEM],
        out_specs=[VMEM, VMEM],
        out_shape=[array(width, 2 * width)] * 2,
        compiler_params=params(12),
        cost_estimate=BRIEF,
        name="pair_gram",
    )(own, neighbour)


def half_rows(place_ref, ref, start, size):
    half = ref.shape[0] // 2
    return ref[pl.ds(pl.multiple_of(place_ref[0] * half, half) + start, size)]


def cross_kernel(start, pieces, adds, place_ref, own_ref, next_ref, *rest):
    out_ref = rest[-1]
    total = rest[2 * pieces][...] if adds else jnp.zeros(out_ref.shape, F32)
    for far_ref, next_far_ref in zip(rest[:pieces], rest[pieces : 2 * pieces]):
        size = min(512, far_ref.shape[0])
        for begin in range(0, far_ref.shape[0], size):
            span = slice(begin, begin + size)
            here = [half_rows(place_ref, ref, start, size) for ref in (own_ref, next_ref)]
            here = split(jnp.concatenate(here, 1))
            there = split(jnp.concatenate([far_ref[span], next_far_ref[span]], 1))
            total += product(here, there, TN)
            start += size
    out_ref[...] = total


def cross_gram(place, own, neighbour, far, next_far, start, before=(), first=()):
    width = own.shape[1]
    return pl.pallas_call(
        functools.partial(cross_kernel, start, len(far), len(before)),
        in_specs=[SMEM] + [VMEM] * (2 + 2 * len(far) + len(before)) + [ANY] * len(first),
        out_specs=VMEM,
        out_shape=array(2 * width, 2 * width),
        compiler_params=params(12),
        cost_estimate=BRIEF,
        name="cross_gram",
    )(place, own, neighbour, *far, *next_far, *before, *first)


def rotations(grams, sign):
    width = grams[0].shape[0]
    half = width // 2
    row = lax.broadcasted_iota(jnp.int32, (width, width), 0)
    column = lax.broadcasted_iota(jnp.int32, (width, width), 1)
    diagonal = (row == column).astype(F32)
    order = jnp.where(row < column, 0.5, -0.5) * (1.0 - diagonal)
    order = jnp.where((row < half) == (column < half), order, order * sign)
    iterates = []
    for gram in grams:
        inverse_row = 1.0 / jnp.sqrt(jnp.sum(gram * diagonal, axis=0, keepdims=True))
        inverse_column = 1.0 / jnp.sqrt(jnp.sum(gram * diagonal, axis=1, keepdims=True))
        skew = gram * inverse_column * inverse_row * order
        iterates.append((diagonal + skew) / jnp.sqrt(1.0 + jnp.sum(skew * skew)))
    for step in range(NS_STEPS):
        parts = [split(iterate) for iterate in iterates]
        squares = [product(part, part, NT) for part in parts]
        rests = [0.5 * (diagonal - square) for square in squares]
        iterates = [
            iterate + product(part, split(rest), NN)
            for iterate, part, rest in zip(iterates, parts, rests)
        ]
    return iterates


def symmetric(first, cross, second):
    return jnp.concatenate(
        [jnp.concatenate([first, cross], 1), jnp.concatenate([cross.T, second], 1)], 0
    )


def turn_kernel(
    place_ref, top_ref, bottom_ref, far_top_ref, far_bottom_ref, cross_ref, far_cross_ref, kept_ref,
    turned_ref, norm_ref,
):
    width = top_ref.shape[0]
    sign_far = jnp.where(place_ref[0] == 0, 1.0, -1.0)
    sign_next = jnp.where(place_ref[1] == 0, 1.0, -1.0)
    cross = cross_ref[...] + far_cross_ref[...].T
    top, bottom, far_top, far_bottom = top_ref[...], bottom_ref[...], far_top_ref[...], far_bottom_ref[...]
    lo, hi = slice(0, width), slice(width, 2 * width)
    gram_01 = symmetric(top[:, lo], cross[lo, lo], far_top[:, lo])
    gram_23 = symmetric(bottom[:, hi], cross[hi, hi], far_bottom[:, lo])
    mixed = jnp.concatenate(
        [
            jnp.concatenate([top[:, hi], cross[lo, hi]], 1),
            jnp.concatenate([cross[hi, lo].T, far_top[:, hi]], 1),
        ],
        0,
    )
    turn_01, turn_23 = rotations([gram_01, gram_23], sign_far)
    s_01, s_23 = split(turn_01), split(turn_23)
    s_01t, s_23t = split(turn_01.T), split(turn_23.T)
    half_01 = split(product(split(gram_01), s_01, NN))
    half_23 = split(product(split(gram_23), s_23, NN))
    half_mixed = split(product(split(mixed), s_23, NN))

    def corner(left, right, which):
        return product([p[which] for p in left], [p[:, which] for p in right], NN)

    grams = [
        symmetric(corner(s_01t, half_01, w), corner(s_01t, half_mixed, w), corner(s_23t, half_23, w))
        for w in (lo, hi)
    ]
    seconds = rotations(grams, sign_next)

    total = jnp.zeros((1, 1), F32)
    for number, (gram, second, which) in enumerate(zip(grams, seconds, (lo, hi))):
        parts = split(second)
        moved = product(split(gram), parts, NN) * second
        kept = jnp.concatenate([kept_ref[number : number + 1], kept_ref[number + 2 : number + 3]], 1)
        total += jnp.sum(jnp.sum(moved, axis=0, keepdims=True) * kept, axis=1, keepdims=True)
        turned_ref[number] = jnp.concatenate(
            [
                product([p[:, which] for p in s_01], [p[lo, lo] for p in parts], NN),
                product([p[:, which] for p in s_23], [p[hi, lo] for p in parts], NN),
            ],
            0,
        )
    norm_ref[...] = jnp.broadcast_to(total, norm_ref.shape)


def turn(place, grams, kept):
    width = grams[0].shape[0]
    return pl.pallas_call(
        turn_kernel,
        in_specs=[SMEM] + [VMEM] * 7,
        out_specs=[VMEM, VMEM],
        out_shape=[array(2, 4 * width, width), array(8, width)],
        compiler_params=params(24),
        name="turn",
    )(place, *grams, kept)


def place_kernel(place_ref, turned_ref, route_ref, block_ref, next_ref, *rest):
    far_refs, out_ref = rest[:-1], rest[-1]
    width = block_ref.shape[1]
    placed = []
    for piece in zip(*[split(turned_ref[number]) for number in range(2)]):
        moved = sum(dot(piece[number], route_ref[number].astype(BF16), NN) for number in range(2))
        placed.append(moved.T.astype(BF16))
    left = [piece[:, : 2 * width] for piece in placed]
    right = [piece[:, 2 * width :] for piece in placed]
    pieces = len(far_refs) // 2
    done = 0
    for far_ref, next_far_ref in zip(far_refs[:pieces], far_refs[pieces:]):
        size = min(512, far_ref.shape[0])
        for begin in range(0, far_ref.shape[0], size):
            span = slice(begin, begin + size)
            here = [half_rows(place_ref, ref, done, size) for ref in (block_ref, next_ref)]
            near = split(jnp.concatenate([here[0], far_ref[span]], 1))
            away = split(jnp.concatenate([here[1], next_far_ref[span]], 1))
            out_ref[:, done : done + size] = product(left, near, NT) + product(right, away, NT)
            done += size


def placed(place, turned, routes, own, neighbour, far, next_far):
    width = own.shape[1]
    rows = sum(piece.shape[0] for piece in far)
    return pl.pallas_call(
        place_kernel,
        in_specs=[SMEM] + [VMEM] * (4 + 2 * len(far)),
        out_specs=VMEM,
        out_shape=array(routes.shape[2], rows),
        compiler_params=params(16),
        cost_estimate=pl.CostEstimate(
            flops=48 * rows * width * width, bytes_accessed=16 * rows * width, transcendentals=0
        ),
        name="placed",
    )(place, turned, routes, own, neighbour, *far, *next_far)


def spread_kernel(total, kept_ref, norm_ref, out_ref):
    scale = jnp.sqrt(total / norm_ref[0:1, 0:1])
    for tile in range(out_ref.shape[1]):
        value = kept_ref[:, tile * LANES : (tile + 1) * LANES] * scale
        out_ref[:, tile] = value.reshape(out_ref.shape[0], out_ref.shape[2], LANES)


def spread(kept, norm, total, capacity):
    shape = (kept.shape[0] // capacity, kept.shape[1] // LANES, capacity, LANES)
    return pl.pallas_call(
        functools.partial(spread_kernel, total),
        in_specs=[VMEM, VMEM],
        out_specs=VMEM,
        out_shape=array(*shape),
        compiler_params=params(8),
        name="spread",
    )(kept, norm)


def join_kernel(tiles_ref, out_ref):
    for tile in range(tiles_ref.shape[1]):
        out_ref[:, :, tile * LANES : (tile + 1) * LANES] = tiles_ref[:, tile]


def join(tiles):
    groups, count, capacity, _ = tiles.shape
    return pl.pallas_call(
        join_kernel,
        in_specs=[VMEM],
        out_specs=VMEM,
        out_shape=array(groups, capacity, count * LANES),
        compiler_params=params(8),
        name="join",
    )(tiles)


def from_partner(value, axis, distance):
    pairs = [(source, source ^ distance) for source in range(lax.axis_size(axis))]
    return lax.ppermute(value, axis, pairs)


def route_of(listed, side, groups, width):
    keep, owners = listed[0], listed[1]
    kept = keep.shape[0]
    order = jnp.arange(kept, dtype=jnp.int32)
    same = owners[:, None] == owners[None, :]
    slot = jnp.sum((same & (order[None, :] < order[:, None])).astype(jnp.int32), axis=1)
    capacity = max(2, 2 * kept // groups)
    target = (owners * 2 + side) * capacity + slot
    places = jnp.arange(2 * groups * capacity, dtype=jnp.int32)
    columns = jnp.arange(width, dtype=jnp.int32)
    picked = (keep[:, None] == columns[None, :]).astype(BF16)
    placed = (target[:, None] == places[None, :]).astype(BF16)
    return lax.dot_general(picked, placed, (TN, ((), ())), preferred_element_type=F32)


def on_device(two_site, keep_list, owner_map):
    block = two_site[0]
    rows, width = block.shape
    half = rows // 2
    count, groups = lax.axis_size("bond"), lax.axis_size("site")
    far = count // 2
    position = lax.axis_index("bond")
    upper = position // far
    place = jnp.stack([upper, position & 1]).astype(jnp.int32)

    sizes = piece_sizes(half)
    starts = [(1 - upper) * half + sum(sizes[:number]) for number in range(len(sizes))]
    sent = [
        lax.dynamic_slice_in_dim(block, start, size) for start, size in zip(starts, sizes)
    ]
    neighbour = from_partner(block, "bond", 1)
    far_rows = [from_partner(piece, "bond", far) for piece in sent]
    listed = jnp.stack([keep_list[0], owner_map[0, :, 0]])
    top, bottom = pair_gram(block, neighbour)
    next_rows = [from_partner(piece, "bond", 1) for piece in far_rows]
    far_top = from_partner(top, "bond", far)
    far_bottom = from_partner(far_top, "bond", 1)
    listed = after(far_rows[0], listed)
    listed = jnp.concatenate([listed, from_partner(listed, "bond", far)])
    routes = jnp.stack(
        [
            route_of(listed[:2], upper, groups, width),
            route_of(listed[2:], 1 - upper, groups, width),
        ]
    )
    lists = jnp.concatenate([listed[::2], from_partner(listed[::2], "bond", 1)])
    columns = jnp.arange(width, dtype=jnp.int32)
    kept = jnp.sum((lists[:, :, None] == columns).astype(F32), axis=1)

    last = half - sent[-1].shape[0]
    cross = cross_gram(place, block, neighbour, far_rows[:-1], next_rows[:-1], 0)
    cross = cross_gram(place, block, neighbour, far_rows[-1:], next_rows[-1:], last, (cross,))
    far_cross = from_partner(cross, "bond", far)

    turned, squares = turn(place, (top, bottom, far_top, far_bottom, cross, far_cross), kept)
    outgoing = placed(place, turned, routes, block, neighbour, far_rows, next_rows)
    for distance in [1 << bit for bit in range(1, far.bit_length() - 1)]:
        squares = squares + from_partner(squares, "bond", distance)
    keep_count = keep_list.shape[1]
    capacity = max(2, 2 * keep_count // groups)
    members = [
        [(first + far * side) * groups + site for site in range(groups) for side in range(2)]
        for first in range(far)
    ]
    arrived = lax.all_to_all(
        spread(outgoing, squares, float(rows * count * keep_count), capacity),
        ("bond", "site"),
        split_axis=0,
        concat_axis=0,
        tiled=True,
        axis_index_groups=members,
    )
    joined = join(arrived.reshape(groups, rows // LANES, capacity, LANES))
    return joined.reshape(1, 1, groups, capacity, rows)


def solution(mesh):
    return jax.shard_map(
        on_device,
        mesh=mesh,
        in_specs=(P("site", None, "bond"), P("site", "bond"), P("site", "bond", None)),
        out_specs=P("site", "bond", None, None, None),
        check_vma=False,
    )
```

```python
import functools

import jax
import jax.numpy as jnp
from jax import lax
from jax.experimental import pallas as pl
from jax.experimental.pallas import tpu as pltpu
from jax.sharding import PartitionSpec as P

NS_STEPS = 5
LANES = 128
F32 = jnp.float32
BF16 = jnp.bfloat16

NN = ((1,), (0,))
NT = ((1,), (1,))
TN = ((0,), (0,))


def piece_sizes(rows):
    first = rows * 7 // 16
    return (first, rows - first)


def tiles(rows):
    count = max(1, round(rows / 512))
    bounds = [LANES * (number * (rows // LANES) // count) for number in range(count)] + [rows]
    return [slice(begin, end) for begin, end in zip(bounds[:-1], bounds[1:])]


def split(value):
    high = value.astype(BF16)
    return high, (value - high.astype(F32)).astype(BF16)


def dot(left, right, contract):
    return lax.dot_general(left, right, (contract, ((), ())), preferred_element_type=F32)


def product(left, right, contract):
    return dot(left[0], right[0], contract) + (
        dot(left[0], right[1], contract) + dot(left[1], right[0], contract)
    )


VMEM = pl.BlockSpec(memory_space=pltpu.VMEM)
SMEM = pl.BlockSpec(memory_space=pltpu.SMEM)
ANY = pl.BlockSpec(memory_space=pl.ANY)


def array(*shape):
    return jax.ShapeDtypeStruct(shape, F32)


BRIEF = pl.CostEstimate(flops=1, bytes_accessed=1, transcendentals=0)


def params(mebibytes):
    return pltpu.CompilerParams(vmem_limit_bytes=mebibytes * 1024 * 1024)


def held_kernel(first_ref, value_ref, listed_ref, out_ref):
    rows = value_ref.shape[0]
    out_ref[:rows] = value_ref[...]
    out_ref[rows:] = listed_ref[...]


def held(first, value, listed):
    return pl.pallas_call(
        held_kernel,
        in_specs=[ANY, VMEM, VMEM],
        out_specs=VMEM,
        out_shape=array(value.shape[0] + listed.shape[0], value.shape[1]),
        compiler_params=params(8),
        cost_estimate=BRIEF,
        name="held",
    )(first, value, listed)


def half_rows(place_ref, ref, start, size):
    half = ref.shape[0] // 2
    return ref[pl.ds(pl.multiple_of(place_ref[0] * half, half) + start, size)]


def cross_products(place_ref, own_ref, next_ref, far_ref, next_far_ref, start, count):
    width = own_ref.shape[1]
    total = jnp.zeros((2 * width, 2 * width), F32)
    for span in tiles(count):
        first, size = start + span.start, span.stop - span.start
        here = [half_rows(place_ref, ref, first, size) for ref in (own_ref, next_ref)]
        here = split(jnp.concatenate(here, 1))
        there = split(jnp.concatenate([far_ref[span], next_far_ref[span]], 1))
        total += product(here, there, TN)
    lo, hi = slice(0, width), slice(width, 2 * width)
    return [total[lo, lo], total[lo, hi], total[hi, lo], total[hi, hi]]


def first_kernel(place_ref, own_ref, next_ref, far_ref, next_far_ref, out_ref):
    rows, width = own_ref.shape
    chunk = min(1024, rows)
    high = low = jnp.zeros((2 * width, 2 * width), F32)
    for begin in range(0, rows, chunk):
        span = slice(begin, begin + chunk)
        pair = split(jnp.concatenate([own_ref[span], next_ref[span]], 1))
        high += dot(pair[0], pair[0], TN)
        low += dot(pair[0], pair[1], TN)
    gram = high + (low + low.T)
    parts = cross_products(place_ref, own_ref, next_ref, far_ref, next_far_ref, 0, far_ref.shape[0])
    parts += [gram[:width, :width], gram[:width, width:], gram[width:, width:]]
    for number, part in enumerate(parts):
        out_ref[number * width : (number + 1) * width] = part
    out_ref[7 * width :] = jnp.zeros((16, width), F32)


def last_kernel(start, place_ref, own_ref, next_ref, far_ref, next_far_ref, before_ref, out_ref):
    width = own_ref.shape[1]
    count = far_ref.shape[0] - 8
    parts = cross_products(place_ref, own_ref, next_ref, far_ref, next_far_ref, start, count)
    for number, part in enumerate(parts):
        span = slice(number * width, (number + 1) * width)
        out_ref[span] = before_ref[span] + part
    out_ref[4 * width : 7 * width] = before_ref[4 * width : 7 * width]
    out_ref[7 * width : 7 * width + 8] = far_ref[count:]
    out_ref[7 * width + 8 :] = next_far_ref[count:]


def gram_call(kernel, name, place, *values):
    width = values[0].shape[1]
    return pl.pallas_call(
        kernel,
        in_specs=[SMEM] + [VMEM] * len(values),
        out_specs=VMEM,
        out_shape=array(7 * width + 16, width),
        compiler_params=params(12),
        cost_estimate=BRIEF,
        name=name,
    )(place, *values)


def rotations(grams, sign):
    width = grams[0].shape[0]
    half = width // 2
    row = lax.broadcasted_iota(jnp.int32, (width, width), 0)
    column = lax.broadcasted_iota(jnp.int32, (width, width), 1)
    diagonal = (row == column).astype(F32)
    order = jnp.where(row < column, 0.5, -0.5) * (1.0 - diagonal)
    order = jnp.where((row < half) == (column < half), order, order * sign)
    iterates = []
    for gram in grams:
        inverse_row = 1.0 / jnp.sqrt(jnp.sum(gram * diagonal, axis=0, keepdims=True))
        inverse_column = 1.0 / jnp.sqrt(jnp.sum(gram * diagonal, axis=1, keepdims=True))
        skew = gram * inverse_column * inverse_row * order
        iterates.append((diagonal + skew) / jnp.sqrt(1.0 + jnp.sum(skew * skew)))
    for step in range(NS_STEPS):
        parts = [split(iterate) for iterate in iterates]
        squares = [product(part, part, NT) for part in parts]
        rests = [0.5 * (diagonal - square) for square in squares]
        iterates = [
            iterate + product(part, split(rest), NN)
            for iterate, part, rest in zip(iterates, parts, rests)
        ]
    return iterates


def symmetric(first, cross, second):
    return jnp.concatenate(
        [jnp.concatenate([first, cross], 1), jnp.concatenate([cross.T, second], 1)], 0
    )


def kept_row(listed):
    width = listed.shape[1]
    row = lax.broadcasted_iota(jnp.int32, (width // 2, width), 0)
    column = lax.broadcasted_iota(jnp.int32, (width // 2, width), 1)
    numbers = jnp.sum(jnp.where(row == column, listed, 0.0), axis=1, keepdims=True)
    return jnp.sum((numbers == column.astype(F32)).astype(F32), axis=0, keepdims=True)


def turn_kernel(place_ref, mine_ref, theirs_ref, turned_ref, norm_ref):
    width = mine_ref.shape[1]
    sign_far = jnp.where(place_ref[0] == 0, 1.0, -1.0)
    sign_next = jnp.where(place_ref[1] == 0, 1.0, -1.0)
    mine, theirs = [
        [ref[number * width : (number + 1) * width] for number in range(7)]
        for ref in (mine_ref, theirs_ref)
    ]
    lists = [ref[begin : begin + 1] for begin in (7 * width, 7 * width + 8) for ref in (mine_ref, theirs_ref)]
    kept_rows = [kept_row(listed) for listed in lists]
    lo, hi = slice(0, width), slice(width, 2 * width)
    gram_01 = symmetric(mine[4], mine[0] + theirs[0].T, theirs[4])
    gram_23 = symmetric(mine[6], mine[3] + theirs[3].T, theirs[6])
    gram_03 = mine[1] + theirs[2].T
    gram_12 = mine[2].T + theirs[1]
    mixed = jnp.concatenate(
        [jnp.concatenate([mine[5], gram_03], 1), jnp.concatenate([gram_12, theirs[5]], 1)], 0
    )
    turn_01, turn_23 = rotations([gram_01, gram_23], sign_far)
    s_01, s_23 = split(turn_01), split(turn_23)
    s_01t, s_23t = split(turn_01.T), split(turn_23.T)
    half_01 = split(product(split(gram_01), s_01, NN))
    half_23 = split(product(split(gram_23), s_23, NN))
    half_mixed = split(product(split(mixed), s_23, NN))

    def corner(left, right, which):
        return product([p[which] for p in left], [p[:, which] for p in right], NN)

    grams = [
        symmetric(corner(s_01t, half_01, w), corner(s_01t, half_mixed, w), corner(s_23t, half_23, w))
        for w in (lo, hi)
    ]
    seconds = rotations(grams, sign_next)

    total = jnp.zeros((1, 1), F32)
    for number, (gram, second, which) in enumerate(zip(grams, seconds, (lo, hi))):
        parts = split(second)
        moved = product(split(gram), parts, NN) * second
        kept = jnp.concatenate([kept_rows[number], kept_rows[number + 2]], 1)
        total += jnp.sum(jnp.sum(moved, axis=0, keepdims=True) * kept, axis=1, keepdims=True)
        turned_ref[number] = jnp.concatenate(
            [
                product([p[:, which] for p in s_01], [p[lo, lo] for p in parts], NN),
                product([p[:, which] for p in s_23], [p[hi, lo] for p in parts], NN),
            ],
            0,
        )
    norm_ref[...] = jnp.broadcast_to(total, norm_ref.shape)


def turn(place, *values):
    width = values[0].shape[1]
    return pl.pallas_call(
        turn_kernel,
        in_specs=[SMEM] + [VMEM] * len(values),
        out_specs=[VMEM, VMEM],
        out_shape=[array(2, 4 * width, width), array(8, width)],
        compiler_params=params(24),
        name="turn",
    )(place, *values)


def place_kernel(sizes, place_ref, turned_ref, route_ref, block_ref, next_ref, *rest):
    far_refs, out_ref = rest[:-1], rest[-1]
    width = block_ref.shape[1]
    placed = []
    for piece in zip(*[split(turned_ref[number]) for number in range(2)]):
        moved = sum(dot(piece[number], route_ref[number].astype(BF16), NN) for number in range(2))
        placed.append(moved.T.astype(BF16))
    left = [piece[:, : 2 * width] for piece in placed]
    right = [piece[:, 2 * width :] for piece in placed]
    pieces = len(far_refs) // 2
    done = 0
    for far_ref, next_far_ref, rows in zip(far_refs[:pieces], far_refs[pieces:], sizes):
        for span in tiles(rows):
            size = span.stop - span.start
            here = [half_rows(place_ref, ref, done, size) for ref in (block_ref, next_ref)]
            near = split(jnp.concatenate([here[0], far_ref[span]], 1))
            away = split(jnp.concatenate([here[1], next_far_ref[span]], 1))
            out_ref[:, done : done + size] = product(left, near, NT) + product(right, away, NT)
            done += size


def placed(place, turned, routes, own, neighbour, far, next_far, sizes):
    width = own.shape[1]
    rows = sum(sizes)
    return pl.pallas_call(
        functools.partial(place_kernel, sizes),
        in_specs=[SMEM] + [VMEM] * (4 + 2 * len(far)),
        out_specs=VMEM,
        out_shape=array(routes.shape[2], rows),
        compiler_params=params(16),
        cost_estimate=pl.CostEstimate(
            flops=48 * rows * width * width, bytes_accessed=16 * rows * width, transcendentals=0
        ),
        name="placed",
    )(place, turned, routes, own, neighbour, *far, *next_far)


def spread_kernel(total, kept_ref, norm_ref, out_ref):
    scale = jnp.sqrt(total / norm_ref[0:1, 0:1])
    for tile in range(out_ref.shape[1]):
        value = kept_ref[:, tile * LANES : (tile + 1) * LANES] * scale
        out_ref[:, tile] = value.reshape(out_ref.shape[0], out_ref.shape[2], LANES)


def spread(kept, norm, total, capacity):
    shape = (kept.shape[0] // capacity, kept.shape[1] // LANES, capacity, LANES)
    return pl.pallas_call(
        functools.partial(spread_kernel, total),
        in_specs=[VMEM, VMEM],
        out_specs=VMEM,
        out_shape=array(*shape),
        compiler_params=params(8),
        name="spread",
    )(kept, norm)


def join_kernel(tiles_ref, out_ref):
    for tile in range(tiles_ref.shape[1]):
        out_ref[:, :, tile * LANES : (tile + 1) * LANES] = tiles_ref[:, tile]


def join(tiles):
    groups, count, capacity, _ = tiles.shape
    return pl.pallas_call(
        join_kernel,
        in_specs=[VMEM],
        out_specs=VMEM,
        out_shape=array(groups, capacity, count * LANES),
        compiler_params=params(8),
        name="join",
    )(tiles)


def from_partner(value, axis, distance):
    pairs = [(source, source ^ distance) for source in range(lax.axis_size(axis))]
    return lax.ppermute(value, axis, pairs)


def route_of(listed, side, groups):
    width = listed.shape[0]
    kept = width // 2
    keep, owners = listed.astype(jnp.int32).reshape(2, kept)
    order = jnp.arange(kept, dtype=jnp.int32)
    same = owners[:, None] == owners[None, :]
    slot = jnp.sum((same & (order[None, :] < order[:, None])).astype(jnp.int32), axis=1)
    capacity = max(2, 2 * kept // groups)
    target = (owners * 2 + side) * capacity + slot
    places = jnp.arange(2 * groups * capacity, dtype=jnp.int32)
    columns = jnp.arange(width, dtype=jnp.int32)
    picked = (keep[:, None] == columns[None, :]).astype(BF16)
    placed = (target[:, None] == places[None, :]).astype(BF16)
    return lax.dot_general(picked, placed, (TN, ((), ())), preferred_element_type=F32)


def on_device(two_site, keep_list, owner_map):
    block = two_site[0]
    rows, width = block.shape
    half = rows // 2
    count, groups = lax.axis_size("bond"), lax.axis_size("site")
    far = count // 2
    position = lax.axis_index("bond")
    upper = position // far
    place = jnp.stack([upper, position & 1]).astype(jnp.int32)

    sizes = piece_sizes(half)
    starts = [(1 - upper) * half + sum(sizes[:number]) for number in range(len(sizes))]
    listed = jnp.concatenate([keep_list[0], owner_map[0, :, 0]]).astype(F32)
    listed = jnp.broadcast_to(listed, (8, width))
    sources = (block, lax.optimization_barrier(block))
    sent = [
        lax.dynamic_slice_in_dim(source, start, size)
        for source, start, size in zip(sources, starts, sizes)
    ]
    neighbour = from_partner(block, "bond", 1)
    far_a, far_b = [from_partner(piece, "bond", far) for piece in sent]
    next_far_a = from_partner(far_a, "bond", 1)
    grams = gram_call(first_kernel, "first_gram", place, block, neighbour, far_a, next_far_a)
    far_b = held(grams, far_b, listed)
    next_far_b = from_partner(far_b, "bond", 1)
    grams = gram_call(
        functools.partial(last_kernel, sizes[0]),
        "last_gram", place, block, neighbour, far_b, next_far_b, grams,
    )
    far_grams = from_partner(grams, "bond", far)
    routes = jnp.stack(
        [
            route_of(listed[0], upper, groups),
            route_of(far_grams[7 * width], 1 - upper, groups),
        ]
    )

    turned, squares = turn(place, grams, far_grams)
    outgoing = placed(
        place, turned, routes, block, neighbour, (far_a, far_b), (next_far_a, next_far_b), sizes
    )
    for distance in [1 << bit for bit in range(1, far.bit_length() - 1)]:
        squares = squares + from_partner(squares, "bond", distance)
    keep_count = keep_list.shape[1]
    capacity = max(2, 2 * keep_count // groups)
    members = [
        [(first + far * side) * groups + site for site in range(groups) for side in range(2)]
        for first in range(far)
    ]
    arrived = lax.all_to_all(
        spread(outgoing, squares, float(rows * count * keep_count), capacity),
        ("bond", "site"),
        split_axis=0,
        concat_axis=0,
        tiled=True,
        axis_index_groups=members,
    )
    joined = join(arrived.reshape(groups, rows // LANES, capacity, LANES))
    return joined.reshape(1, 1, groups, capacity, rows)


def solution(mesh):
    return jax.shard_map(
        on_device,
        mesh=mesh,
        in_specs=(P("site", None, "bond"), P("site", "bond"), P("site", "bond", None)),
        out_specs=P("site", "bond", None, None, None),
        check_vma=False,
    )
```

```python
import functools

import jax
import jax.numpy as jnp
from jax import lax
from jax.experimental import pallas as pl
from jax.experimental.pallas import tpu as pltpu
from jax.sharding import PartitionSpec as P

NS_STEPS = 5
LANES = 128
F32 = jnp.float32
BF16 = jnp.bfloat16

NN = ((1,), (0,))
NT = ((1,), (1,))
TN = ((0,), (0,))


def piece_sizes(rows):
    first = rows * 3 // 4
    return (first, rows - first)


def tiles(rows):
    count = max(1, round(rows / 512))
    bounds = [LANES * (number * (rows // LANES) // count) for number in range(count)] + [rows]
    return [slice(begin, end) for begin, end in zip(bounds[:-1], bounds[1:])]


def split(value):
    high = value.astype(BF16)
    return high, (value - high.astype(F32)).astype(BF16)


def dot(left, right, contract):
    return lax.dot_general(left, right, (contract, ((), ())), preferred_element_type=F32)


def product(left, right, contract):
    return dot(left[0], right[0], contract) + (
        dot(left[0], right[1], contract) + dot(left[1], right[0], contract)
    )


VMEM = pl.BlockSpec(memory_space=pltpu.VMEM)
SMEM = pl.BlockSpec(memory_space=pltpu.SMEM)
ANY = pl.BlockSpec(memory_space=pl.ANY)


def array(*shape):
    return jax.ShapeDtypeStruct(shape, F32)


BRIEF = pl.CostEstimate(flops=1, bytes_accessed=1, transcendentals=0)


def params(mebibytes):
    return pltpu.CompilerParams(vmem_limit_bytes=mebibytes * 1024 * 1024)


def half_rows(place_ref, ref, start, size):
    half = ref.shape[0] // 2
    return ref[pl.ds(pl.multiple_of(place_ref[0] * half, half) + start, size)]


def cross_products(place_ref, own_ref, next_ref, far_ref, start):
    rows, width = far_ref.shape
    total = jnp.zeros((width, 2 * width), F32)
    for span in tiles(rows):
        first, size = start + span.start, span.stop - span.start
        here = [half_rows(place_ref, ref, first, size) for ref in (own_ref, next_ref)]
        total += product(split(far_ref[span]), split(jnp.concatenate(here, 1)), TN)
    return total


def first_kernel(place_ref, own_ref, next_ref, far_ref, listed_ref, out_ref):
    rows, width = own_ref.shape
    chunk = min(1024, rows)
    total = jnp.zeros((width, 2 * width), F32)
    for begin in range(0, rows, chunk):
        span = slice(begin, begin + chunk)
        own, neighbour = split(own_ref[span]), split(next_ref[span])
        pair = [jnp.concatenate([a, b], 1) for a, b in zip(own, neighbour)]
        total += product(own, pair, TN)
    cross = cross_products(place_ref, own_ref, next_ref, far_ref, 0)
    for number, part in enumerate([cross, total]):
        out_ref[2 * number * width : (2 * number + 1) * width] = part[:, :width]
        out_ref[(2 * number + 1) * width : (2 * number + 2) * width] = part[:, width:]
    out_ref[4 * width :] = listed_ref[...]


def last_kernel(start, place_ref, own_ref, next_ref, far_ref, before_ref, out_ref):
    width = own_ref.shape[1]
    cross = cross_products(place_ref, own_ref, next_ref, far_ref, start)
    out_ref[:width] = before_ref[:width] + cross[:, :width]
    out_ref[width : 2 * width] = before_ref[width : 2 * width] + cross[:, width:]
    out_ref[2 * width :] = before_ref[2 * width :]


def gram_call(kernel, name, place, *values):
    width = values[0].shape[1]
    return pl.pallas_call(
        kernel,
        in_specs=[SMEM] + [VMEM] * len(values),
        out_specs=VMEM,
        out_shape=array(4 * width + 8, width),
        compiler_params=params(12),
        cost_estimate=BRIEF,
        name=name,
    )(place, *values)


def rotations(grams, sign):
    width = grams[0].shape[0]
    half = width // 2
    row = lax.broadcasted_iota(jnp.int32, (width, width), 0)
    column = lax.broadcasted_iota(jnp.int32, (width, width), 1)
    diagonal = (row == column).astype(F32)
    order = jnp.where(row < column, 0.5, -0.5) * (1.0 - diagonal)
    order = jnp.where((row < half) == (column < half), order, order * sign)
    iterates = []
    for gram in grams:
        inverse_row = 1.0 / jnp.sqrt(jnp.sum(gram * diagonal, axis=0, keepdims=True))
        inverse_column = 1.0 / jnp.sqrt(jnp.sum(gram * diagonal, axis=1, keepdims=True))
        skew = gram * inverse_column * inverse_row * order
        iterates.append((diagonal + skew) / jnp.sqrt(1.0 + jnp.sum(skew * skew)))
    for step in range(NS_STEPS):
        parts = [split(iterate) for iterate in iterates]
        squares = [product(part, part, NT) for part in parts]
        rests = [0.5 * (diagonal - square) for square in squares]
        iterates = [
            iterate + product(part, split(rest), NN)
            for iterate, part, rest in zip(iterates, parts, rests)
        ]
    return iterates


def symmetric(first, cross, second):
    return jnp.concatenate(
        [jnp.concatenate([first, cross], 1), jnp.concatenate([cross.T, second], 1)], 0
    )


def kept_row(listed):
    width = listed.shape[1]
    row = lax.broadcasted_iota(jnp.int32, (width // 2, width), 0)
    column = lax.broadcasted_iota(jnp.int32, (width // 2, width), 1)
    numbers = jnp.sum(jnp.where(row == column, listed, 0.0), axis=1, keepdims=True)
    return jnp.sum((numbers == column.astype(F32)).astype(F32), axis=0, keepdims=True)


def turn_kernel(place_ref, mine_ref, far_ref, next_ref, next_far_ref, turned_ref, norm_ref):
    width = mine_ref.shape[1]
    sign_far = jnp.where(place_ref[0] == 0, 1.0, -1.0)
    sign_next = jnp.where(place_ref[1] == 0, 1.0, -1.0)
    refs = (mine_ref, far_ref, next_ref, next_far_ref)
    mine, far, neighbour, next_far = [
        [ref[number * width : (number + 1) * width] for number in range(4)] for ref in refs
    ]
    kept_rows = [kept_row(ref[4 * width : 4 * width + 1]) for ref in refs]
    lo, hi = slice(0, width), slice(width, 2 * width)
    gram_01 = symmetric(mine[2], mine[0].T + far[0], far[2])
    gram_23 = symmetric(neighbour[2], neighbour[0].T + next_far[0], next_far[2])
    gram_03 = far[1] + neighbour[1].T
    gram_12 = mine[1] + next_far[1].T
    mixed = jnp.concatenate(
        [jnp.concatenate([mine[3], gram_03], 1), jnp.concatenate([gram_12, far[3]], 1)], 0
    )
    turn_01, turn_23 = rotations([gram_01, gram_23], sign_far)
    s_01, s_23 = split(turn_01), split(turn_23)
    s_01t, s_23t = split(turn_01.T), split(turn_23.T)
    half_01 = split(product(split(gram_01), s_01, NN))
    half_23 = split(product(split(gram_23), s_23, NN))
    half_mixed = split(product(split(mixed), s_23, NN))

    def corner(left, right, which):
        return product([p[which] for p in left], [p[:, which] for p in right], NN)

    grams = [
        symmetric(corner(s_01t, half_01, w), corner(s_01t, half_mixed, w), corner(s_23t, half_23, w))
        for w in (lo, hi)
    ]
    seconds = rotations(grams, sign_next)

    total = jnp.zeros((1, 1), F32)
    for number, (gram, second, which) in enumerate(zip(grams, seconds, (lo, hi))):
        parts = split(second)
        moved = product(split(gram), parts, NN) * second
        kept = jnp.concatenate([kept_rows[number], kept_rows[number + 2]], 1)
        total += jnp.sum(jnp.sum(moved, axis=0, keepdims=True) * kept, axis=1, keepdims=True)
        turned_ref[number] = jnp.concatenate(
            [
                product([p[:, which] for p in s_01], [p[lo, lo] for p in parts], NN),
                product([p[:, which] for p in s_23], [p[hi, lo] for p in parts], NN),
            ],
            0,
        )
    norm_ref[...] = jnp.broadcast_to(total, norm_ref.shape)


def turn(place, *values):
    width = values[0].shape[1]
    return pl.pallas_call(
        turn_kernel,
        in_specs=[SMEM] + [VMEM] * len(values),
        out_specs=[VMEM, VMEM],
        out_shape=[array(2, 4 * width, width), array(8, width)],
        compiler_params=params(24),
        name="turn",
    )(place, *values)


def place_kernel(sizes, place_ref, turned_ref, route_ref, block_ref, next_ref, *rest):
    far_refs, out_ref = rest[:-1], rest[-1]
    width = block_ref.shape[1]
    moved = []
    for piece in zip(*[split(turned_ref[number]) for number in range(2)]):
        total = sum(dot(piece[number], route_ref[number].astype(BF16), NN) for number in range(2))
        moved.append(total.astype(BF16))
    top = [piece[: 2 * width] for piece in moved]
    bottom = [piece[2 * width :] for piece in moved]
    pieces = len(far_refs) // 2
    done = 0
    for far_ref, next_far_ref, rows in zip(far_refs[:pieces], far_refs[pieces:], sizes):
        for span in tiles(rows):
            size = span.stop - span.start
            here = [half_rows(place_ref, ref, done, size) for ref in (block_ref, next_ref)]
            near = split(jnp.concatenate([here[0], far_ref[span]], 1))
            away = split(jnp.concatenate([here[1], next_far_ref[span]], 1))
            out_ref[:, done : done + size] = (product(near, top, NN) + product(away, bottom, NN)).T
            done += size


def placed(place, turned, routes, own, neighbour, far, next_far, sizes):
    width = own.shape[1]
    rows = sum(sizes)
    return pl.pallas_call(
        functools.partial(place_kernel, sizes),
        in_specs=[SMEM] + [VMEM] * (4 + 2 * len(far)),
        out_specs=VMEM,
        out_shape=array(routes.shape[2], rows),
        compiler_params=params(16),
        cost_estimate=pl.CostEstimate(
            flops=48 * rows * width * width, bytes_accessed=16 * rows * width, transcendentals=0
        ),
        name="placed",
    )(place, turned, routes, own, neighbour, *far, *next_far)


def spread_kernel(total, kept_ref, norm_ref, out_ref):
    scale = jnp.sqrt(total / norm_ref[0:1, 0:1])
    for tile in range(out_ref.shape[1]):
        value = kept_ref[:, tile * LANES : (tile + 1) * LANES] * scale
        out_ref[:, tile] = value.reshape(out_ref.shape[0], out_ref.shape[2], LANES)


def spread(kept, norm, total, capacity):
    shape = (kept.shape[0] // capacity, kept.shape[1] // LANES, capacity, LANES)
    return pl.pallas_call(
        functools.partial(spread_kernel, total),
        in_specs=[VMEM, VMEM],
        out_specs=VMEM,
        out_shape=array(*shape),
        compiler_params=params(8),
        name="spread",
    )(kept, norm)


def join_kernel(tiles_ref, out_ref):
    for tile in range(tiles_ref.shape[1]):
        out_ref[:, :, tile * LANES : (tile + 1) * LANES] = tiles_ref[:, tile]


def join(tiles):
    groups, count, capacity, _ = tiles.shape
    return pl.pallas_call(
        join_kernel,
        in_specs=[VMEM],
        out_specs=VMEM,
        out_shape=array(groups, capacity, count * LANES),
        compiler_params=params(8),
        name="join",
    )(tiles)


def from_partner(value, axis, distance):
    pairs = [(source, source ^ distance) for source in range(lax.axis_size(axis))]
    return lax.ppermute(value, axis, pairs)


def route_of(listed, side, groups):
    width = listed.shape[0]
    kept = width // 2
    keep, owners = listed.astype(jnp.int32).reshape(2, kept)
    order = jnp.arange(kept, dtype=jnp.int32)
    same = owners[:, None] == owners[None, :]
    slot = jnp.sum((same & (order[None, :] < order[:, None])).astype(jnp.int32), axis=1)
    capacity = max(2, 2 * kept // groups)
    target = (owners * 2 + side) * capacity + slot
    places = jnp.arange(2 * groups * capacity, dtype=jnp.int32)
    columns = jnp.arange(width, dtype=jnp.int32)
    picked = (keep[:, None] == columns[None, :]).astype(BF16)
    placed = (target[:, None] == places[None, :]).astype(BF16)
    return lax.dot_general(picked, placed, (TN, ((), ())), preferred_element_type=F32)


def on_device(two_site, keep_list, owner_map):
    block = two_site[0]
    rows, width = block.shape
    half = rows // 2
    count, groups = lax.axis_size("bond"), lax.axis_size("site")
    far = count // 2
    position = lax.axis_index("bond")
    upper = position // far
    place = jnp.stack([upper, position & 1]).astype(jnp.int32)

    sizes = piece_sizes(half)
    starts = [(1 - upper) * half + sum(sizes[:number]) for number in range(len(sizes))]
    listed = jnp.concatenate([keep_list[0], owner_map[0, :, 0]]).astype(F32)
    listed = jnp.broadcast_to(listed, (8, width))
    sources = (block, lax.optimization_barrier(block))
    sent = [
        lax.dynamic_slice_in_dim(source, start, size)
        for source, start, size in zip(sources, starts, sizes)
    ]
    neighbour = from_partner(block, "bond", 1)
    far_a, far_b = [from_partner(piece, "bond", far) for piece in sent]
    grams = gram_call(first_kernel, "first_gram", place, block, neighbour, far_a, listed)
    grams = gram_call(
        functools.partial(last_kernel, sizes[0]),
        "last_gram", place, block, neighbour, far_b, grams,
    )
    far_grams = from_partner(grams, "bond", far)
    next_grams = [from_partner(value, "bond", 1) for value in (grams, far_grams)]
    next_far_a, next_far_b = [from_partner(value, "bond", 1) for value in (far_a, far_b)]
    routes = jnp.stack(
        [
            route_of(listed[0], upper, groups),
            route_of(far_grams[4 * width], 1 - upper, groups),
        ]
    )

    turned, squares = turn(place, grams, far_grams, *next_grams)
    outgoing = placed(
        place, turned, routes, block, neighbour, (far_a, far_b), (next_far_a, next_far_b), sizes
    )
    for distance in [1 << bit for bit in range(1, far.bit_length() - 1)]:
        squares = squares + from_partner(squares, "bond", distance)
    keep_count = keep_list.shape[1]
    capacity = max(2, 2 * keep_count // groups)
    members = [
        [(first + far * side) * groups + site for site in range(groups) for side in range(2)]
        for first in range(far)
    ]
    arrived = lax.all_to_all(
        spread(outgoing, squares, float(rows * count * keep_count), capacity),
        ("bond", "site"),
        split_axis=0,
        concat_axis=0,
        tiled=True,
        axis_index_groups=members,
    )
    joined = join(arrived.reshape(groups, rows // LANES, capacity, LANES))
    return joined.reshape(1, 1, groups, capacity, rows)


def solution(mesh):
    return jax.shard_map(
        on_device,
        mesh=mesh,
        in_specs=(P("site", None, "bond"), P("site", "bond"), P("site", "bond", None)),
        out_specs=P("site", "bond", None, None, None),
        check_vma=False,
    )
```

```python
import functools

import jax
import jax.numpy as jnp
from jax import lax
from jax.experimental import pallas as pl
from jax.experimental.pallas import tpu as pltpu
from jax.sharding import PartitionSpec as P

NS_STEPS = 5
LANES = 128
F32 = jnp.float32
BF16 = jnp.bfloat16

NN = ((1,), (0,))
NT = ((1,), (1,))
TN = ((0,), (0,))


def piece_sizes(rows):
    first = rows * 3 // 4
    return (first, rows - first)


def tiles(rows):
    count = max(1, round(rows / 512))
    bounds = [LANES * (number * (rows // LANES) // count) for number in range(count)] + [rows]
    return [slice(begin, end) for begin, end in zip(bounds[:-1], bounds[1:])]


def split(value):
    high = value.astype(BF16)
    return high, (value - high.astype(F32)).astype(BF16)


def dot(left, right, contract):
    return lax.dot_general(left, right, (contract, ((), ())), preferred_element_type=F32)


def product(left, right, contract):
    return dot(left[0], right[0], contract) + (
        dot(left[0], right[1], contract) + dot(left[1], right[0], contract)
    )


VMEM = pl.BlockSpec(memory_space=pltpu.VMEM)
SMEM = pl.BlockSpec(memory_space=pltpu.SMEM)
ANY = pl.BlockSpec(memory_space=pl.ANY)


def array(*shape):
    return jax.ShapeDtypeStruct(shape, F32)


BRIEF = pl.CostEstimate(flops=1, bytes_accessed=1, transcendentals=0)


def params(mebibytes):
    return pltpu.CompilerParams(vmem_limit_bytes=mebibytes * 1024 * 1024)


def half_rows(place_ref, ref, start, size):
    half = ref.shape[0] // 2
    return ref[pl.ds(pl.multiple_of(place_ref[0] * half, half) + start, size)]


def half_rows_of(place_ref, refs, start, size):
    rows = refs[0].shape[0]
    side = len(refs) // 2
    piece, first = start // rows, start % rows
    span = slice(first, first + size)
    return jnp.where(place_ref[0] == 0, refs[piece][span], refs[side + piece][span])


def cross_products(place_ref, own_ref, next_refs, far_ref, start):
    rows, width = far_ref.shape
    total = jnp.zeros((width, 2 * width), F32)
    for span in tiles(rows):
        first, size = start + span.start, span.stop - span.start
        here = [
            half_rows(place_ref, own_ref, first, size),
            half_rows_of(place_ref, next_refs, first, size),
        ]
        total += product(split(far_ref[span]), split(jnp.concatenate(here, 1)), TN)
    return total


def first_kernel(place_ref, own_ref, far_ref, listed_ref, *rest):
    next_refs, out_ref = rest[:-1], rest[-1]
    rows, width = own_ref.shape
    chunk = rows // len(next_refs)
    total = jnp.zeros((width, 2 * width), F32)
    for number, next_ref in enumerate(next_refs):
        span = slice(number * chunk, (number + 1) * chunk)
        own, neighbour = split(own_ref[span]), split(next_ref[...])
        pair = [jnp.concatenate([a, b], 1) for a, b in zip(own, neighbour)]
        total += product(own, pair, TN)
    cross = cross_products(place_ref, own_ref, next_refs, far_ref, 0)
    for number, part in enumerate([cross, total]):
        out_ref[2 * number * width : (2 * number + 1) * width] = part[:, :width]
        out_ref[(2 * number + 1) * width : (2 * number + 2) * width] = part[:, width:]
    out_ref[4 * width :] = listed_ref[...]


def last_kernel(start, place_ref, own_ref, far_ref, before_ref, *rest):
    next_refs, out_ref = rest[:-1], rest[-1]
    width = own_ref.shape[1]
    cross = cross_products(place_ref, own_ref, next_refs, far_ref, start)
    out_ref[:width] = before_ref[:width] + cross[:, :width]
    out_ref[width : 2 * width] = before_ref[width : 2 * width] + cross[:, width:]
    out_ref[2 * width :] = before_ref[2 * width :]


def gram_call(kernel, name, place, *values):
    width = values[0].shape[1]
    return pl.pallas_call(
        kernel,
        in_specs=[SMEM] + [VMEM] * len(values),
        out_specs=VMEM,
        out_shape=array(4 * width + 8, width),
        compiler_params=params(12),
        cost_estimate=BRIEF,
        name=name,
    )(place, *values)


def rotations(grams, sign):
    width = grams[0].shape[0]
    half = width // 2
    row = lax.broadcasted_iota(jnp.int32, (width, width), 0)
    column = lax.broadcasted_iota(jnp.int32, (width, width), 1)
    diagonal = (row == column).astype(F32)
    order = jnp.where(row < column, 0.5, -0.5) * (1.0 - diagonal)
    order = jnp.where((row < half) == (column < half), order, order * sign)
    iterates = []
    for gram in grams:
        inverse_row = 1.0 / jnp.sqrt(jnp.sum(gram * diagonal, axis=0, keepdims=True))
        inverse_column = 1.0 / jnp.sqrt(jnp.sum(gram * diagonal, axis=1, keepdims=True))
        skew = gram * inverse_column * inverse_row * order
        iterates.append((diagonal + skew) / jnp.sqrt(1.0 + jnp.sum(skew * skew)))
    for step in range(NS_STEPS):
        parts = [split(iterate) for iterate in iterates]
        squares = [product(part, part, NT) for part in parts]
        rests = [0.5 * (diagonal - square) for square in squares]
        iterates = [
            iterate + product(part, split(rest), NN)
            for iterate, part, rest in zip(iterates, parts, rests)
        ]
    return iterates


def symmetric(first, cross, second):
    return jnp.concatenate(
        [jnp.concatenate([first, cross], 1), jnp.concatenate([cross.T, second], 1)], 0
    )


def kept_row(listed):
    width = listed.shape[1]
    row = lax.broadcasted_iota(jnp.int32, (width // 2, width), 0)
    column = lax.broadcasted_iota(jnp.int32, (width // 2, width), 1)
    numbers = jnp.sum(jnp.where(row == column, listed, 0.0), axis=1, keepdims=True)
    return jnp.sum((numbers == column.astype(F32)).astype(F32), axis=0, keepdims=True)


def turn_kernel(place_ref, mine_ref, far_ref, next_ref, next_far_ref, turned_ref, norm_ref):
    width = mine_ref.shape[1]
    sign_far = jnp.where(place_ref[0] == 0, 1.0, -1.0)
    sign_next = jnp.where(place_ref[1] == 0, 1.0, -1.0)
    refs = (mine_ref, far_ref, next_ref, next_far_ref)
    mine, far, neighbour, next_far = [
        [ref[number * width : (number + 1) * width] for number in range(4)] for ref in refs
    ]
    kept_rows = [kept_row(ref[4 * width : 4 * width + 1]) for ref in refs]
    lo, hi = slice(0, width), slice(width, 2 * width)
    gram_01 = symmetric(mine[2], mine[0].T + far[0], far[2])
    gram_23 = symmetric(neighbour[2], neighbour[0].T + next_far[0], next_far[2])
    gram_03 = far[1] + neighbour[1].T
    gram_12 = mine[1] + next_far[1].T
    mixed = jnp.concatenate(
        [jnp.concatenate([mine[3], gram_03], 1), jnp.concatenate([gram_12, far[3]], 1)], 0
    )
    turn_01, turn_23 = rotations([gram_01, gram_23], sign_far)
    s_01, s_23 = split(turn_01), split(turn_23)
    s_01t, s_23t = split(turn_01.T), split(turn_23.T)
    half_01 = split(product(split(gram_01), s_01, NN))
    half_23 = split(product(split(gram_23), s_23, NN))
    half_mixed = split(product(split(mixed), s_23, NN))

    def corner(left, right, which):
        return product([p[which] for p in left], [p[:, which] for p in right], NN)

    grams = [
        symmetric(corner(s_01t, half_01, w), corner(s_01t, half_mixed, w), corner(s_23t, half_23, w))
        for w in (lo, hi)
    ]
    seconds = rotations(grams, sign_next)

    total = jnp.zeros((1, 1), F32)
    for number, (gram, second, which) in enumerate(zip(grams, seconds, (lo, hi))):
        parts = split(second)
        moved = product(split(gram), parts, NN) * second
        kept = jnp.concatenate([kept_rows[number], kept_rows[number + 2]], 1)
        total += jnp.sum(jnp.sum(moved, axis=0, keepdims=True) * kept, axis=1, keepdims=True)
        turned_ref[number] = jnp.concatenate(
            [
                product([p[:, which] for p in s_01], [p[lo, lo] for p in parts], NN),
                product([p[:, which] for p in s_23], [p[hi, lo] for p in parts], NN),
            ],
            0,
        )
    norm_ref[...] = jnp.broadcast_to(total, norm_ref.shape)


def turn(place, *values):
    width = values[0].shape[1]
    return pl.pallas_call(
        turn_kernel,
        in_specs=[SMEM] + [VMEM] * len(values),
        out_specs=[VMEM, VMEM],
        out_shape=[array(2, 4 * width, width), array(8, width)],
        compiler_params=params(24),
        name="turn",
    )(place, *values)


def place_kernel(spans, count, place_ref, turned_ref, route_ref, block_ref, *rest):
    next_refs, rest = rest[:count], rest[count:]
    far_refs, next_far_refs, out_ref = rest[: len(spans)], rest[len(spans) : 2 * len(spans)], rest[-1]
    width = block_ref.shape[1]
    moved = []
    for piece in zip(*[split(turned_ref[number]) for number in range(2)]):
        total = sum(dot(piece[number], route_ref[number].astype(BF16), NN) for number in range(2))
        moved.append(total.astype(BF16))
    top = [piece[: 2 * width] for piece in moved]
    bottom = [piece[2 * width :] for piece in moved]
    done = 0
    for far_ref, next_far_ref, (start, span) in zip(far_refs, next_far_refs, spans):
        for tile in tiles(span.stop - span.start):
            size = tile.stop - tile.start
            there = slice(span.start + tile.start, span.start + tile.stop)
            here = [
                half_rows(place_ref, block_ref, start + tile.start, size),
                half_rows_of(place_ref, next_refs, start + tile.start, size),
            ]
            near = split(jnp.concatenate([here[0], far_ref[there]], 1))
            away = split(jnp.concatenate([here[1], next_far_ref[there]], 1))
            out_ref[:, done : done + size] = (product(near, top, NN) + product(away, bottom, NN)).T
            done += size


def placed(place, turned, routes, own, neighbour, far, next_far, spans, first=()):
    width = own.shape[1]
    rows = sum(span.stop - span.start for _, span in spans)
    return pl.pallas_call(
        functools.partial(place_kernel, spans, len(neighbour)),
        in_specs=[SMEM] + [VMEM] * (3 + len(neighbour) + 2 * len(far)) + [ANY] * len(first),
        out_specs=VMEM,
        out_shape=array(routes.shape[2], rows),
        compiler_params=params(16),
        cost_estimate=pl.CostEstimate(
            flops=48 * rows * width * width, bytes_accessed=16 * rows * width, transcendentals=0
        ),
        name="placed",
    )(place, turned, routes, own, *neighbour, *far, *next_far, *first)


def spread_kernel(total, *refs):
    norm_ref, out_ref = refs[-2:]
    scale = jnp.sqrt(total / norm_ref[0:1, 0:1])
    done = 0
    for ref in refs[:-2]:
        for tile in range(ref.shape[1] // LANES):
            value = ref[:, tile * LANES : (tile + 1) * LANES] * scale
            out_ref[:, done] = value.reshape(out_ref.shape[0], out_ref.shape[2], LANES)
            done += 1


def spread(values, norm, total, capacity):
    count = sum(value.shape[1] for value in values) // LANES
    return pl.pallas_call(
        functools.partial(spread_kernel, total),
        in_specs=[VMEM] * (len(values) + 1),
        out_specs=VMEM,
        out_shape=array(values[0].shape[0] // capacity, count, capacity, LANES),
        compiler_params=params(8),
        name="spread",
    )(*values, norm)


def join_kernel(tiles_ref, out_ref):
    for member, site in enumerate(member_order(tiles_ref.shape[0])):
        for tile in range(tiles_ref.shape[1]):
            out_ref[site, :, tile * LANES : (tile + 1) * LANES] = tiles_ref[member, tile]


def join(tiles):
    groups, count, capacity, _ = tiles.shape
    return pl.pallas_call(
        join_kernel,
        in_specs=[VMEM],
        out_specs=VMEM,
        out_shape=array(groups, capacity, count * LANES),
        compiler_params=params(8),
        name="join",
    )(tiles)


def from_partner(value, axis, distance):
    pairs = [(source, source ^ distance) for source in range(lax.axis_size(axis))]
    return lax.ppermute(value, axis, pairs)


def member_order(groups):
    if groups % 32:
        return list(range(groups))
    return [
        16 * high + 8 * low + z
        for high in range(groups // 16)
        for z in range(8)
        for low in range(2)
    ]


def route_of(listed, side, groups):
    width = listed.shape[0]
    kept = width // 2
    keep, owners = listed.astype(jnp.int32).reshape(2, kept)
    order = jnp.arange(kept, dtype=jnp.int32)
    same = owners[:, None] == owners[None, :]
    slot = jnp.sum((same & (order[None, :] < order[:, None])).astype(jnp.int32), axis=1)
    capacity = max(2, 2 * kept // groups)
    order_of = member_order(groups)
    rank = jnp.array([order_of.index(site) for site in range(groups)], jnp.int32)
    ranks = jnp.sum(
        jnp.where(owners[:, None] == jnp.arange(groups, dtype=jnp.int32), rank, 0), axis=1
    )
    target = (ranks * 2 + side) * capacity + slot
    places = jnp.arange(2 * groups * capacity, dtype=jnp.int32)
    columns = jnp.arange(width, dtype=jnp.int32)
    picked = (keep[:, None] == columns[None, :]).astype(BF16)
    placed = (target[:, None] == places[None, :]).astype(BF16)
    return lax.dot_general(picked, placed, (TN, ((), ())), preferred_element_type=F32)


def on_device(two_site, keep_list, owner_map):
    block = two_site[0]
    rows, width = block.shape
    half = rows // 2
    count, groups = lax.axis_size("bond"), lax.axis_size("site")
    far = count // 2
    position = lax.axis_index("bond")
    upper = position // far
    place = jnp.stack([upper, position & 1]).astype(jnp.int32)

    sizes = piece_sizes(half)
    starts = [(1 - upper) * half + sum(sizes[:number]) for number in range(len(sizes))]
    listed = jnp.concatenate([keep_list[0], owner_map[0, :, 0]]).astype(F32)
    listed = jnp.broadcast_to(listed, (8, width))
    sources = (block, lax.optimization_barrier(block))
    sent = [
        lax.dynamic_slice_in_dim(source, start, size)
        for source, start, size in zip(sources, starts, sizes)
    ]
    quarter = rows // 4
    neighbour = [
        from_partner(block[number * quarter : (number + 1) * quarter], "bond", 1)
        for number in range(4)
    ]
    far_a, far_b = [from_partner(piece, "bond", far) for piece in sent]
    grams = gram_call(first_kernel, "first_gram", place, block, far_a, listed, *neighbour)
    grams = gram_call(
        functools.partial(last_kernel, sizes[0]),
        "last_gram", place, block, far_b, grams, *neighbour,
    )
    far_grams = from_partner(grams, "bond", far)
    next_grams = [from_partner(value, "bond", 1) for value in (grams, far_grams)]
    next_far_a, next_far_b = [from_partner(value, "bond", 1) for value in (far_a, far_b)]
    routes = jnp.stack(
        [
            route_of(listed[0], upper, groups),
            route_of(far_grams[4 * width], 1 - upper, groups),
        ]
    )

    turned, squares = turn(place, grams, far_grams, *next_grams)
    middle = sizes[0] * 2 // 3
    outgoing = [
        placed(
            place, turned, routes, block, neighbour, (far_a,), (next_far_a,),
            ((0, slice(0, middle)),),
        )
    ]
    squares = squares + from_partner(squares, "bond", 2)
    outgoing.append(
        placed(
            place, turned, routes, block, neighbour, (far_a, far_b), (next_far_a, next_far_b),
            ((middle, slice(middle, sizes[0])), (sizes[0], slice(0, sizes[1]))), (squares,),
        )
    )
    for distance in [1 << bit for bit in range(2, far.bit_length() - 1)]:
        squares = squares + from_partner(squares, "bond", distance)
    keep_count = keep_list.shape[1]
    capacity = max(2, 2 * keep_count // groups)
    order = member_order(groups)
    members = [
        [(first + far * side) * groups + site for site in order for side in range(2)]
        for first in range(far)
    ]
    arrived = lax.all_to_all(
        spread(outgoing, squares, float(rows * count * keep_count), capacity),
        ("bond", "site"),
        split_axis=0,
        concat_axis=0,
        tiled=True,
        axis_index_groups=members,
    )
    joined = join(arrived.reshape(groups, rows // LANES, capacity, LANES))
    return joined.reshape(1, 1, groups, capacity, rows)


def solution(mesh):
    return jax.shard_map(
        on_device,
        mesh=mesh,
        in_specs=(P("site", None, "bond"), P("site", "bond"), P("site", "bond", None)),
        out_specs=P("site", "bond", None, None, None),
        check_vma=False,
    )
```

```python
import functools

import jax
import jax.numpy as jnp
from jax import lax
from jax.experimental import pallas as pl
from jax.experimental.pallas import tpu as pltpu
from jax.sharding import PartitionSpec as P

NS_STEPS = 5
LANES = 128
F32 = jnp.float32
BF16 = jnp.bfloat16

NN = ((1,), (0,))
NT = ((1,), (1,))
TN = ((0,), (0,))


def piece_sizes(rows):
    first = rows * 3 // 4
    return (first, rows - first)


def tiles(rows):
    count = max(1, round(rows / 512))
    bounds = [LANES * (number * (rows // LANES) // count) for number in range(count)] + [rows]
    return [slice(begin, end) for begin, end in zip(bounds[:-1], bounds[1:])]


def split(value):
    high = value.astype(BF16)
    return high, (value - high.astype(F32)).astype(BF16)


def dot(left, right, contract):
    return lax.dot_general(left, right, (contract, ((), ())), preferred_element_type=F32)


def product(left, right, contract):
    return dot(left[0], right[0], contract) + (
        dot(left[0], right[1], contract) + dot(left[1], right[0], contract)
    )


VMEM = pl.BlockSpec(memory_space=pltpu.VMEM)
SMEM = pl.BlockSpec(memory_space=pltpu.SMEM)
ANY = pl.BlockSpec(memory_space=pl.ANY)


def array(*shape):
    return jax.ShapeDtypeStruct(shape, F32)


BRIEF = pl.CostEstimate(flops=1, bytes_accessed=1, transcendentals=0)


def params(mebibytes):
    return pltpu.CompilerParams(vmem_limit_bytes=mebibytes * 1024 * 1024)


def half_rows(place_ref, ref, start, size):
    half = ref.shape[0] // 2
    return ref[pl.ds(pl.multiple_of(place_ref[0] * half, half) + start, size)]


def half_rows_of(place_ref, refs, start, size):
    rows = refs[0].shape[0]
    side = len(refs) // 2
    piece, first = start // rows, start % rows
    span = slice(first, first + size)
    return jnp.where(place_ref[0] == 0, refs[piece][span], refs[side + piece][span])


def cross_products(place_ref, own_ref, next_refs, far_ref, start):
    rows, width = far_ref.shape
    total = jnp.zeros((width, 2 * width), F32)
    for span in tiles(rows):
        first, size = start + span.start, span.stop - span.start
        here = [
            half_rows(place_ref, own_ref, first, size),
            half_rows_of(place_ref, next_refs, first, size),
        ]
        total += product(split(far_ref[span]), split(jnp.concatenate(here, 1)), TN)
    return total


def first_kernel(place_ref, own_ref, far_ref, listed_ref, *rest):
    next_refs, out_ref = rest[:-1], rest[-1]
    rows, width = own_ref.shape
    chunk = rows // len(next_refs)
    total = jnp.zeros((width, 2 * width), F32)
    for number, next_ref in enumerate(next_refs):
        span = slice(number * chunk, (number + 1) * chunk)
        own, neighbour = split(own_ref[span]), split(next_ref[...])
        pair = [jnp.concatenate([a, b], 1) for a, b in zip(own, neighbour)]
        total += product(own, pair, TN)
    cross = cross_products(place_ref, own_ref, next_refs, far_ref, 0)
    for number, part in enumerate([cross, total]):
        out_ref[2 * number * width : (2 * number + 1) * width] = part[:, :width]
        out_ref[(2 * number + 1) * width : (2 * number + 2) * width] = part[:, width:]
    out_ref[4 * width :] = listed_ref[...]


def last_kernel(start, place_ref, own_ref, far_ref, before_ref, *rest):
    next_refs, out_ref = rest[:-1], rest[-1]
    width = own_ref.shape[1]
    cross = cross_products(place_ref, own_ref, next_refs, far_ref, start)
    out_ref[:width] = before_ref[:width] + cross[:, :width]
    out_ref[width : 2 * width] = before_ref[width : 2 * width] + cross[:, width:]
    out_ref[2 * width :] = before_ref[2 * width :]


def gram_call(kernel, name, place, *values):
    width = values[0].shape[1]
    return pl.pallas_call(
        kernel,
        in_specs=[SMEM] + [VMEM] * len(values),
        out_specs=VMEM,
        out_shape=array(4 * width + 8, width),
        compiler_params=params(12),
        cost_estimate=BRIEF,
        name=name,
    )(place, *values)


def rotations(grams, sign):
    width = grams[0].shape[0]
    half = width // 2
    row = lax.broadcasted_iota(jnp.int32, (width, width), 0)
    column = lax.broadcasted_iota(jnp.int32, (width, width), 1)
    diagonal = (row == column).astype(F32)
    order = jnp.where(row < column, 0.5, -0.5) * (1.0 - diagonal)
    order = jnp.where((row < half) == (column < half), order, order * sign)
    iterates = []
    for gram in grams:
        inverse_row = 1.0 / jnp.sqrt(jnp.sum(gram * diagonal, axis=0, keepdims=True))
        inverse_column = 1.0 / jnp.sqrt(jnp.sum(gram * diagonal, axis=1, keepdims=True))
        skew = gram * inverse_column * inverse_row * order
        iterates.append((diagonal + skew) / jnp.sqrt(1.0 + jnp.sum(skew * skew)))
    for step in range(NS_STEPS):
        parts = [split(iterate) for iterate in iterates]
        squares = [product(part, part, NT) for part in parts]
        rests = [0.5 * (diagonal - square) for square in squares]
        iterates = [
            iterate + product(part, split(rest), NN)
            for iterate, part, rest in zip(iterates, parts, rests)
        ]
    return iterates


def symmetric(first, cross, second):
    return jnp.concatenate(
        [jnp.concatenate([first, cross], 1), jnp.concatenate([cross.T, second], 1)], 0
    )


def kept_row(listed):
    width = listed.shape[1]
    row = lax.broadcasted_iota(jnp.int32, (width // 2, width), 0)
    column = lax.broadcasted_iota(jnp.int32, (width // 2, width), 1)
    numbers = jnp.sum(jnp.where(row == column, listed, 0.0), axis=1, keepdims=True)
    return jnp.sum((numbers == column.astype(F32)).astype(F32), axis=0, keepdims=True)


def turn_kernel(place_ref, mine_ref, far_ref, next_ref, next_far_ref, turned_ref, norm_ref):
    width = mine_ref.shape[1]
    sign_far = jnp.where(place_ref[0] == 0, 1.0, -1.0)
    sign_next = jnp.where(place_ref[1] == 0, 1.0, -1.0)
    refs = (mine_ref, far_ref, next_ref, next_far_ref)
    mine, far, neighbour, next_far = [
        [ref[number * width : (number + 1) * width] for number in range(4)] for ref in refs
    ]
    kept_rows = [kept_row(ref[4 * width : 4 * width + 1]) for ref in refs]
    lo, hi = slice(0, width), slice(width, 2 * width)
    gram_01 = symmetric(mine[2], mine[0].T + far[0], far[2])
    gram_23 = symmetric(neighbour[2], neighbour[0].T + next_far[0], next_far[2])
    gram_03 = far[1] + neighbour[1].T
    gram_12 = mine[1] + next_far[1].T
    mixed = jnp.concatenate(
        [jnp.concatenate([mine[3], gram_03], 1), jnp.concatenate([gram_12, far[3]], 1)], 0
    )
    turn_01, turn_23 = rotations([gram_01, gram_23], sign_far)
    s_01, s_23 = split(turn_01), split(turn_23)
    s_01t, s_23t = split(turn_01.T), split(turn_23.T)
    half_01 = split(product(split(gram_01), s_01, NN))
    half_23 = split(product(split(gram_23), s_23, NN))
    half_mixed = split(product(split(mixed), s_23, NN))

    def corner(left, right, which):
        return product([p[which] for p in left], [p[:, which] for p in right], NN)

    grams = [
        symmetric(corner(s_01t, half_01, w), corner(s_01t, half_mixed, w), corner(s_23t, half_23, w))
        for w in (lo, hi)
    ]
    seconds = rotations(grams, sign_next)

    total = jnp.zeros((1, 1), F32)
    for number, (gram, second, which) in enumerate(zip(grams, seconds, (lo, hi))):
        parts = split(second)
        moved = product(split(gram), parts, NN) * second
        kept = jnp.concatenate([kept_rows[number], kept_rows[number + 2]], 1)
        total += jnp.sum(jnp.sum(moved, axis=0, keepdims=True) * kept, axis=1, keepdims=True)
        turned_ref[number] = jnp.concatenate(
            [
                product([p[:, which] for p in s_01], [p[lo, lo] for p in parts], NN),
                product([p[:, which] for p in s_23], [p[hi, lo] for p in parts], NN),
            ],
            0,
        )
    norm_ref[...] = jnp.broadcast_to(total, norm_ref.shape)


def turn(place, *values):
    width = values[0].shape[1]
    return pl.pallas_call(
        turn_kernel,
        in_specs=[SMEM] + [VMEM] * len(values),
        out_specs=[VMEM, VMEM],
        out_shape=[array(2, 4 * width, width), array(8, width)],
        compiler_params=params(24),
        name="turn",
    )(place, *values)


def place_kernel(spans, count, place_ref, turned_ref, route_ref, block_ref, *rest):
    next_refs, rest = rest[:count], rest[count:]
    far_refs, next_far_refs, out_ref = rest[: len(spans)], rest[len(spans) : 2 * len(spans)], rest[-1]
    width = block_ref.shape[1]
    moved = []
    for piece in zip(*[split(turned_ref[number]) for number in range(2)]):
        total = sum(dot(piece[number], route_ref[number].astype(BF16), NN) for number in range(2))
        moved.append(total.astype(BF16))
    top = [piece[: 2 * width] for piece in moved]
    bottom = [piece[2 * width :] for piece in moved]
    done = 0
    for far_ref, next_far_ref, (start, span) in zip(far_refs, next_far_refs, spans):
        for tile in tiles(span.stop - span.start):
            size = tile.stop - tile.start
            there = slice(span.start + tile.start, span.start + tile.stop)
            here = [
                half_rows(place_ref, block_ref, start + tile.start, size),
                half_rows_of(place_ref, next_refs, start + tile.start, size),
            ]
            near = split(jnp.concatenate([here[0], far_ref[there]], 1))
            away = split(jnp.concatenate([here[1], next_far_ref[there]], 1))
            out_ref[:, done : done + size] = (product(near, top, NN) + product(away, bottom, NN)).T
            done += size


def placed(place, turned, routes, own, neighbour, far, next_far, spans, first=()):
    width = own.shape[1]
    rows = sum(span.stop - span.start for _, span in spans)
    return pl.pallas_call(
        functools.partial(place_kernel, spans, len(neighbour)),
        in_specs=[SMEM] + [VMEM] * (3 + len(neighbour) + 2 * len(far)) + [ANY] * len(first),
        out_specs=VMEM,
        out_shape=array(routes.shape[2], rows),
        compiler_params=params(16),
        cost_estimate=pl.CostEstimate(
            flops=48 * rows * width * width, bytes_accessed=16 * rows * width, transcendentals=0
        ),
        name="placed",
    )(place, turned, routes, own, *neighbour, *far, *next_far, *first)


def spread_kernel(total, *refs):
    norm_ref, out_ref = refs[-2:]
    scale = jnp.sqrt(total / norm_ref[0:1, 0:1])
    done = 0
    for ref in refs[:-2]:
        for tile in range(ref.shape[1] // LANES):
            value = ref[:, tile * LANES : (tile + 1) * LANES] * scale
            out_ref[:, done] = value.reshape(out_ref.shape[0], out_ref.shape[2], LANES)
            done += 1


def spread(values, norm, total, capacity):
    count = sum(value.shape[1] for value in values) // LANES
    return pl.pallas_call(
        functools.partial(spread_kernel, total),
        in_specs=[VMEM] * (len(values) + 1),
        out_specs=VMEM,
        out_shape=array(values[0].shape[0] // capacity, count, capacity, LANES),
        compiler_params=params(8),
        name="spread",
    )(*values, norm)


def join_kernel(tiles_ref, out_ref):
    for member, site in enumerate(member_order(tiles_ref.shape[0])):
        for tile in range(tiles_ref.shape[1]):
            out_ref[site, :, tile * LANES : (tile + 1) * LANES] = tiles_ref[member, tile]


def join(tiles):
    groups, count, capacity, _ = tiles.shape
    return pl.pallas_call(
        join_kernel,
        in_specs=[VMEM],
        out_specs=VMEM,
        out_shape=array(groups, capacity, count * LANES),
        compiler_params=params(8),
        name="join",
    )(tiles)


def from_partner(value, axis, distance):
    pairs = [(source, source ^ distance) for source in range(lax.axis_size(axis))]
    return lax.ppermute(value, axis, pairs)


def member_order(groups):
    if groups % 32:
        return list(range(groups))
    return [
        16 * high + 8 * low + z
        for high in range(groups // 16)
        for z in range(8)
        for low in range(2)
    ]


def route_of(listed, side, groups):
    width = listed.shape[0]
    kept = width // 2
    keep, owners = listed.astype(jnp.int32).reshape(2, kept)
    order = jnp.arange(kept, dtype=jnp.int32)
    same = owners[:, None] == owners[None, :]
    slot = jnp.sum((same & (order[None, :] < order[:, None])).astype(jnp.int32), axis=1)
    capacity = max(2, 2 * kept // groups)
    order_of = member_order(groups)
    rank = jnp.array([order_of.index(site) for site in range(groups)], jnp.int32)
    ranks = jnp.sum(
        jnp.where(owners[:, None] == jnp.arange(groups, dtype=jnp.int32), rank, 0), axis=1
    )
    target = (ranks * 2 + side) * capacity + slot
    places = jnp.arange(2 * groups * capacity, dtype=jnp.int32)
    columns = jnp.arange(width, dtype=jnp.int32)
    picked = (keep[:, None] == columns[None, :]).astype(BF16)
    placed = (target[:, None] == places[None, :]).astype(BF16)
    return lax.dot_general(picked, placed, (TN, ((), ())), preferred_element_type=F32)


def on_device(two_site, keep_list, owner_map):
    block = two_site[0]
    rows, width = block.shape
    half = rows // 2
    count, groups = lax.axis_size("bond"), lax.axis_size("site")
    far = count // 2
    position = lax.axis_index("bond")
    upper = position // far
    place = jnp.stack([upper, position & 1]).astype(jnp.int32)

    sizes = piece_sizes(half)
    starts = [(1 - upper) * half + sum(sizes[:number]) for number in range(len(sizes))]
    listed = jnp.concatenate([keep_list[0], owner_map[0, :, 0]]).astype(F32)
    listed = jnp.broadcast_to(listed, (8, width))
    sources = (block, lax.optimization_barrier(block))
    sent = [
        lax.dynamic_slice_in_dim(source, start, size)
        for source, start, size in zip(sources, starts, sizes)
    ]
    quarter = rows // 4
    neighbour = [
        from_partner(block[number * quarter : (number + 1) * quarter], "bond", 1)
        for number in range(4)
    ]
    far_a, far_b = [from_partner(piece, "bond", far) for piece in sent]
    grams = gram_call(first_kernel, "first_gram", place, block, far_a, listed, *neighbour)
    grams = gram_call(
        functools.partial(last_kernel, sizes[0]),
        "last_gram", place, block, far_b, grams, *neighbour,
    )
    far_grams = from_partner(grams, "bond", far)
    next_grams = [from_partner(value, "bond", 1) for value in (grams, far_grams)]
    next_far_a, next_far_b = [from_partner(value, "bond", 1) for value in (far_a, far_b)]
    routes = jnp.stack(
        [
            route_of(listed[0], upper, groups),
            route_of(far_grams[4 * width], 1 - upper, groups),
        ]
    )

    turned, squares = turn(place, grams, far_grams, *next_grams)
    outgoing = placed(
        place, turned, routes, block, neighbour, (far_a, far_b), (next_far_a, next_far_b),
        ((0, slice(0, sizes[0])), (sizes[0], slice(0, sizes[1]))),
    )
    for distance in [1 << bit for bit in range(1, far.bit_length() - 1)]:
        squares = squares + from_partner(squares, "bond", distance)
    keep_count = keep_list.shape[1]
    capacity = max(2, 2 * keep_count // groups)
    order = member_order(groups)
    members = [
        [(first + far * side) * groups + site for site in order for side in range(2)]
        for first in range(far)
    ]
    arrived = lax.all_to_all(
        spread([outgoing], squares, float(rows * count * keep_count), capacity),
        ("bond", "site"),
        split_axis=0,
        concat_axis=0,
        tiled=True,
        axis_index_groups=members,
    )
    joined = join(arrived.reshape(groups, rows // LANES, capacity, LANES))
    return joined.reshape(1, 1, groups, capacity, rows)


def solution(mesh):
    return jax.shard_map(
        on_device,
        mesh=mesh,
        in_specs=(P("site", None, "bond"), P("site", "bond"), P("site", "bond", None)),
        out_specs=P("site", "bond", None, None, None),
        check_vma=False,
    )
```

```python
import functools

import jax
import jax.numpy as jnp
from jax import lax
from jax.experimental import pallas as pl
from jax.experimental.pallas import tpu as pltpu
from jax.sharding import PartitionSpec as P

NS_STEPS = 5
LANES = 128
F32 = jnp.float32
BF16 = jnp.bfloat16

NN = ((1,), (0,))
NT = ((1,), (1,))
TN = ((0,), (0,))


def piece_sizes(rows):
    first = rows * 3 // 4
    return (first, rows - first)


def tiles(rows):
    count = max(1, round(rows / 512))
    bounds = [LANES * (number * (rows // LANES) // count) for number in range(count)] + [rows]
    return [slice(begin, end) for begin, end in zip(bounds[:-1], bounds[1:])]


def split(value):
    high = value.astype(BF16)
    return high, (value - high.astype(F32)).astype(BF16)


def dot(left, right, contract):
    return lax.dot_general(left, right, (contract, ((), ())), preferred_element_type=F32)


def product(left, right, contract):
    return dot(left[0], right[0], contract) + (
        dot(left[0], right[1], contract) + dot(left[1], right[0], contract)
    )


VMEM = pl.BlockSpec(memory_space=pltpu.VMEM)
SMEM = pl.BlockSpec(memory_space=pltpu.SMEM)
ANY = pl.BlockSpec(memory_space=pl.ANY)


def array(*shape):
    return jax.ShapeDtypeStruct(shape, F32)


BRIEF = pl.CostEstimate(flops=1, bytes_accessed=1, transcendentals=0)


def params(mebibytes):
    return pltpu.CompilerParams(vmem_limit_bytes=mebibytes * 1024 * 1024)


def half_rows(place_ref, ref, start, size):
    half = ref.shape[0] // 2
    return ref[pl.ds(pl.multiple_of(place_ref[0] * half, half) + start, size)]


def half_rows_of(place_ref, refs, start, size):
    rows = refs[0].shape[0]
    side = len(refs) // 2
    piece, first = start // rows, start % rows
    span = slice(first, first + size)
    return jnp.where(place_ref[0] == 0, refs[piece][span], refs[side + piece][span])


def cross_products(place_ref, own_ref, next_refs, far_ref, start):
    rows, width = far_ref.shape
    total = jnp.zeros((width, 2 * width), F32)
    for span in tiles(rows):
        first, size = start + span.start, span.stop - span.start
        here = [
            half_rows(place_ref, own_ref, first, size),
            half_rows_of(place_ref, next_refs, first, size),
        ]
        total += product(split(far_ref[span]), split(jnp.concatenate(here, 1)), TN)
    return total


def first_kernel(place_ref, own_ref, far_ref, listed_ref, *rest):
    next_refs, out_ref = rest[:-1], rest[-1]
    rows, width = own_ref.shape
    chunk = rows // len(next_refs)
    total = jnp.zeros((width, 2 * width), F32)
    for number, next_ref in enumerate(next_refs):
        span = slice(number * chunk, (number + 1) * chunk)
        own, neighbour = split(own_ref[span]), split(next_ref[...])
        pair = [jnp.concatenate([a, b], 1) for a, b in zip(own, neighbour)]
        total += product(own, pair, TN)
    cross = cross_products(place_ref, own_ref, next_refs, far_ref, 0)
    for number, part in enumerate([cross, total]):
        out_ref[2 * number * width : (2 * number + 1) * width] = part[:, :width]
        out_ref[(2 * number + 1) * width : (2 * number + 2) * width] = part[:, width:]
    out_ref[4 * width :] = listed_ref[...]


def last_kernel(start, place_ref, own_ref, far_ref, before_ref, *rest):
    next_refs, out_ref = rest[:-1], rest[-1]
    width = own_ref.shape[1]
    cross = cross_products(place_ref, own_ref, next_refs, far_ref, start)
    out_ref[:width] = before_ref[:width] + cross[:, :width]
    out_ref[width : 2 * width] = before_ref[width : 2 * width] + cross[:, width:]
    out_ref[2 * width :] = before_ref[2 * width :]


def gram_call(kernel, name, place, *values):
    width = values[0].shape[1]
    return pl.pallas_call(
        kernel,
        in_specs=[SMEM] + [VMEM] * len(values),
        out_specs=VMEM,
        out_shape=array(4 * width + 8, width),
        compiler_params=params(12),
        cost_estimate=BRIEF,
        name=name,
    )(place, *values)


def rotations(grams, sign):
    width = grams[0].shape[0]
    half = width // 2
    row = lax.broadcasted_iota(jnp.int32, (width, width), 0)
    column = lax.broadcasted_iota(jnp.int32, (width, width), 1)
    diagonal = (row == column).astype(F32)
    order = jnp.where(row < column, 0.5, -0.5) * (1.0 - diagonal)
    order = jnp.where((row < half) == (column < half), order, order * sign)
    iterates = []
    for gram in grams:
        inverse_row = 1.0 / jnp.sqrt(jnp.sum(gram * diagonal, axis=0, keepdims=True))
        inverse_column = 1.0 / jnp.sqrt(jnp.sum(gram * diagonal, axis=1, keepdims=True))
        skew = gram * inverse_column * inverse_row * order
        iterates.append((diagonal + skew) / jnp.sqrt(1.0 + jnp.sum(skew * skew)))
    for step in range(NS_STEPS):
        parts = [split(iterate) for iterate in iterates]
        squares = [product(part, part, NT) for part in parts]
        rests = [0.5 * (diagonal - square) for square in squares]
        iterates = [
            iterate + product(part, split(rest), NN)
            for iterate, part, rest in zip(iterates, parts, rests)
        ]
    return iterates


def symmetric(first, cross, second):
    return jnp.concatenate(
        [jnp.concatenate([first, cross], 1), jnp.concatenate([cross.T, second], 1)], 0
    )


def kept_row(listed):
    width = listed.shape[1]
    row = lax.broadcasted_iota(jnp.int32, (width // 2, width), 0)
    column = lax.broadcasted_iota(jnp.int32, (width // 2, width), 1)
    numbers = jnp.sum(jnp.where(row == column, listed, 0.0), axis=1, keepdims=True)
    return jnp.sum((numbers == column.astype(F32)).astype(F32), axis=0, keepdims=True)


def turn_kernel(place_ref, mine_ref, far_ref, next_ref, next_far_ref, first_ref, second_ref, norm_ref):
    width = mine_ref.shape[1]
    sign_far = jnp.where(place_ref[0] == 0, 1.0, -1.0)
    sign_next = jnp.where(place_ref[1] == 0, 1.0, -1.0)
    refs = (mine_ref, far_ref, next_ref, next_far_ref)
    mine, far, neighbour, next_far = [
        [ref[number * width : (number + 1) * width] for number in range(4)] for ref in refs
    ]
    kept_rows = [kept_row(ref[4 * width : 4 * width + 1]) for ref in refs]
    lo, hi = slice(0, width), slice(width, 2 * width)
    gram_01 = symmetric(mine[2], mine[0].T + far[0], far[2])
    gram_23 = symmetric(neighbour[2], neighbour[0].T + next_far[0], next_far[2])
    gram_03 = far[1] + neighbour[1].T
    gram_12 = mine[1] + next_far[1].T
    mixed = jnp.concatenate(
        [jnp.concatenate([mine[3], gram_03], 1), jnp.concatenate([gram_12, far[3]], 1)], 0
    )
    turn_01, turn_23 = rotations([gram_01, gram_23], sign_far)
    s_01, s_23 = split(turn_01), split(turn_23)
    s_01t, s_23t = split(turn_01.T), split(turn_23.T)
    half_01 = split(product(split(gram_01), s_01, NN))
    half_23 = split(product(split(gram_23), s_23, NN))
    half_mixed = split(product(split(mixed), s_23, NN))

    def corner(left, right, which):
        return product([p[which] for p in left], [p[:, which] for p in right], NN)

    grams = [
        symmetric(corner(s_01t, half_01, w), corner(s_01t, half_mixed, w), corner(s_23t, half_23, w))
        for w in (lo, hi)
    ]
    seconds = rotations(grams, sign_next)

    first_ref[0], first_ref[1] = turn_01, turn_23
    total = jnp.zeros((1, 1), F32)
    for number, (gram, second) in enumerate(zip(grams, seconds)):
        second_ref[number] = second[:, :width]
        moved = product(split(gram), split(second), NN) * second
        kept = jnp.concatenate([kept_rows[number], kept_rows[number + 2]], 1)
        total += jnp.sum(jnp.sum(moved, axis=0, keepdims=True) * kept, axis=1, keepdims=True)
    norm_ref[...] = jnp.broadcast_to(total, norm_ref.shape)


def turn(place, *values):
    width = values[0].shape[1]
    return pl.pallas_call(
        turn_kernel,
        in_specs=[SMEM] + [VMEM] * len(values),
        out_specs=[VMEM] * 3,
        out_shape=[
            array(2, 2 * width, 2 * width),
            array(2, 2 * width, width),
            array(8, width),
        ],
        compiler_params=params(24),
        name="turn",
    )(place, *values)


def route_kernel(first_ref, second_ref, route_ref, high_ref, low_ref):
    width = second_ref.shape[2]
    firsts = [split(first_ref[number]) for number in range(2)]
    totals = [0.0, 0.0]
    for number in range(2):
        second = split(second_ref[number])
        which = slice(number * width, (number + 1) * width)
        turned = jnp.concatenate(
            [
                product(
                    [piece[:, which] for piece in first],
                    [piece[side * width : (side + 1) * width] for piece in second],
                    NN,
                )
                for side, first in enumerate(firsts)
            ],
            0,
        )
        route = route_ref[number].astype(BF16)
        totals = [total + dot(piece, route, NN) for total, piece in zip(totals, split(turned))]
    high_ref[...] = totals[0].astype(BF16)
    low_ref[...] = totals[1].astype(BF16)


def routed(first, second, routes):
    shape = jax.ShapeDtypeStruct((2 * first.shape[1], routes.shape[2]), BF16)
    return pl.pallas_call(
        route_kernel,
        in_specs=[VMEM] * 3,
        out_specs=[VMEM] * 2,
        out_shape=[shape, shape],
        compiler_params=params(12),
        cost_estimate=BRIEF,
        name="routed",
    )(first, second, routes)


def sum_kernel(left_ref, right_ref, *rest):
    rest[-1][...] = left_ref[...] + right_ref[...]


def sum_after(left, right, *first):
    return pl.pallas_call(
        sum_kernel,
        in_specs=[VMEM, VMEM] + [ANY] * len(first),
        out_specs=VMEM,
        out_shape=array(*left.shape),
        compiler_params=params(8),
        cost_estimate=BRIEF,
        name="sum_after",
    )(left, right, *first)


def place_kernel(spans, count, place_ref, high_ref, low_ref, block_ref, *rest):
    next_refs, rest = rest[:count], rest[count:]
    far_refs, next_far_refs, out_ref = rest[: len(spans)], rest[len(spans) : 2 * len(spans)], rest[-1]
    width = block_ref.shape[1]
    top, bottom = [
        [ref[side * 2 * width : (side + 1) * 2 * width] for ref in (high_ref, low_ref)]
        for side in range(2)
    ]
    done = 0
    for far_ref, next_far_ref, (start, span) in zip(far_refs, next_far_refs, spans):
        for tile in tiles(span.stop - span.start):
            size = tile.stop - tile.start
            there = slice(span.start + tile.start, span.start + tile.stop)
            here = [
                half_rows(place_ref, block_ref, start + tile.start, size),
                half_rows_of(place_ref, next_refs, start + tile.start, size),
            ]
            near = split(jnp.concatenate([here[0], far_ref[there]], 1))
            away = split(jnp.concatenate([here[1], next_far_ref[there]], 1))
            out_ref[:, done : done + size] = (product(near, top, NN) + product(away, bottom, NN)).T
            done += size


def placed(place, parts, own, neighbour, far, next_far, spans):
    width = own.shape[1]
    rows = sum(span.stop - span.start for _, span in spans)
    return pl.pallas_call(
        functools.partial(place_kernel, spans, len(neighbour)),
        in_specs=[SMEM] + [VMEM] * (3 + len(neighbour) + 2 * len(far)),
        out_specs=VMEM,
        out_shape=array(parts[0].shape[1], rows),
        compiler_params=params(16),
        cost_estimate=pl.CostEstimate(
            flops=48 * rows * width * width, bytes_accessed=16 * rows * width, transcendentals=0
        ),
        name="placed",
    )(place, *parts, own, *neighbour, *far, *next_far)


def spread_kernel(total, *refs):
    norm_ref, other_ref, out_ref = refs[-3:]
    scale = jnp.sqrt(total / (norm_ref[0:1, 0:1] + other_ref[0:1, 0:1]))
    done = 0
    for ref in refs[:-3]:
        for tile in range(ref.shape[1] // LANES):
            value = ref[:, tile * LANES : (tile + 1) * LANES] * scale
            out_ref[:, done] = value.reshape(out_ref.shape[0], out_ref.shape[2], LANES)
            done += 1


def spread(values, norms, total, capacity):
    count = sum(value.shape[1] for value in values) // LANES
    return pl.pallas_call(
        functools.partial(spread_kernel, total),
        in_specs=[VMEM] * (len(values) + 2),
        out_specs=VMEM,
        out_shape=array(values[0].shape[0] // capacity, count, capacity, LANES),
        compiler_params=params(8),
        name="spread",
    )(*values, *norms)


def join_kernel(tiles_ref, out_ref):
    for member, site in enumerate(member_order(tiles_ref.shape[0])):
        for tile in range(tiles_ref.shape[1]):
            out_ref[site, :, tile * LANES : (tile + 1) * LANES] = tiles_ref[member, tile]


def join(tiles):
    groups, count, capacity, _ = tiles.shape
    return pl.pallas_call(
        join_kernel,
        in_specs=[VMEM],
        out_specs=VMEM,
        out_shape=array(groups, capacity, count * LANES),
        compiler_params=params(8),
        name="join",
    )(tiles)


def from_partner(value, axis, distance):
    pairs = [(source, source ^ distance) for source in range(lax.axis_size(axis))]
    return lax.ppermute(value, axis, pairs)


def member_order(groups):
    if groups % 32:
        return list(range(groups))
    return [
        16 * high + 8 * low + z
        for high in range(groups // 16)
        for z in range(8)
        for low in range(2)
    ]


def route_of(listed, side, groups):
    width = listed.shape[0]
    kept = width // 2
    keep, owners = listed.astype(jnp.int32).reshape(2, kept)
    order = jnp.arange(kept, dtype=jnp.int32)
    same = owners[:, None] == owners[None, :]
    slot = jnp.sum((same & (order[None, :] < order[:, None])).astype(jnp.int32), axis=1)
    capacity = max(2, 2 * kept // groups)
    order_of = member_order(groups)
    rank = jnp.array([order_of.index(site) for site in range(groups)], jnp.int32)
    ranks = jnp.sum(
        jnp.where(owners[:, None] == jnp.arange(groups, dtype=jnp.int32), rank, 0), axis=1
    )
    target = (ranks * 2 + side) * capacity + slot
    places = jnp.arange(2 * groups * capacity, dtype=jnp.int32)
    columns = jnp.arange(width, dtype=jnp.int32)
    picked = (keep[:, None] == columns[None, :]).astype(BF16)
    placed = (target[:, None] == places[None, :]).astype(BF16)
    return lax.dot_general(picked, placed, (TN, ((), ())), preferred_element_type=F32)


def on_device(two_site, keep_list, owner_map):
    block = two_site[0]
    rows, width = block.shape
    half = rows // 2
    count, groups = lax.axis_size("bond"), lax.axis_size("site")
    far = count // 2
    position = lax.axis_index("bond")
    upper = position // far
    place = jnp.stack([upper, position & 1]).astype(jnp.int32)

    sizes = piece_sizes(half)
    starts = [(1 - upper) * half + sum(sizes[:number]) for number in range(len(sizes))]
    listed = jnp.concatenate([keep_list[0], owner_map[0, :, 0]]).astype(F32)
    listed = jnp.broadcast_to(listed, (8, width))
    sources = (block, lax.optimization_barrier(block))
    sent = [
        lax.dynamic_slice_in_dim(source, start, size)
        for source, start, size in zip(sources, starts, sizes)
    ]
    quarter = rows // 4
    neighbour = [
        from_partner(block[number * quarter : (number + 1) * quarter], "bond", 1)
        for number in range(4)
    ]
    far_a, far_b = [from_partner(piece, "bond", far) for piece in sent]
    grams = gram_call(first_kernel, "first_gram", place, block, far_a, listed, *neighbour)
    grams = gram_call(
        functools.partial(last_kernel, sizes[0]),
        "last_gram", place, block, far_b, grams, *neighbour,
    )
    far_grams = from_partner(grams, "bond", far)
    next_grams = [from_partner(value, "bond", 1) for value in (grams, far_grams)]
    next_far_a, next_far_b = [from_partner(value, "bond", 1) for value in (far_a, far_b)]
    routes = jnp.stack(
        [
            route_of(listed[0], upper, groups),
            route_of(far_grams[4 * width], 1 - upper, groups),
        ]
    )

    first, second, squares = turn(place, grams, far_grams, *next_grams)
    parts = routed(first, second, routes)
    squares = sum_after(
        squares, from_partner(squares, "bond", 2), parts[0], next_far_a, next_far_b
    )
    outgoing = placed(
        place, parts, block, neighbour, (far_a, far_b), (next_far_a, next_far_b),
        ((0, slice(0, sizes[0])), (sizes[0], slice(0, sizes[1]))),
    )
    norms = (squares, from_partner(squares, "bond", 4))
    keep_count = keep_list.shape[1]
    capacity = max(2, 2 * keep_count // groups)
    order = member_order(groups)
    members = [
        [(first + far * side) * groups + site for site in order for side in range(2)]
        for first in range(far)
    ]
    arrived = lax.all_to_all(
        spread([outgoing], norms, float(rows * count * keep_count), capacity),
        ("bond", "site"),
        split_axis=0,
        concat_axis=0,
        tiled=True,
        axis_index_groups=members,
    )
    joined = join(arrived.reshape(groups, rows // LANES, capacity, LANES))
    return joined.reshape(1, 1, groups, capacity, rows)


def solution(mesh):
    return jax.shard_map(
        on_device,
        mesh=mesh,
        in_specs=(P("site", None, "bond"), P("site", "bond"), P("site", "bond", None)),
        out_specs=P("site", "bond", None, None, None),
        check_vma=False,
    )
```

```python
import functools

import jax
import jax.numpy as jnp
from jax import lax
from jax.experimental import pallas as pl
from jax.experimental.pallas import tpu as pltpu
from jax.sharding import PartitionSpec as P

NS_STEPS = 5
LANES = 128
F32 = jnp.float32
BF16 = jnp.bfloat16

NN = ((1,), (0,))
NT = ((1,), (1,))
TN = ((0,), (0,))


def piece_sizes(rows):
    first = rows * 3 // 4
    return (first, rows - first)


def tiles(rows):
    count = max(1, round(rows / 512))
    bounds = [LANES * (number * (rows // LANES) // count) for number in range(count)] + [rows]
    return [slice(begin, end) for begin, end in zip(bounds[:-1], bounds[1:])]


def split(value):
    high = value.astype(BF16)
    return high, (value - high.astype(F32)).astype(BF16)


def dot(left, right, contract):
    return lax.dot_general(left, right, (contract, ((), ())), preferred_element_type=F32)


def product(left, right, contract):
    (along_left,), (along_right,) = contract
    return dot(
        jnp.concatenate([left[0], left[0], left[1]], along_left),
        jnp.concatenate([right[0], right[1], right[0]], along_right),
        contract,
    )


VMEM = pl.BlockSpec(memory_space=pltpu.VMEM)
SMEM = pl.BlockSpec(memory_space=pltpu.SMEM)
ANY = pl.BlockSpec(memory_space=pl.ANY)


def array(*shape):
    return jax.ShapeDtypeStruct(shape, F32)


BRIEF = pl.CostEstimate(flops=1, bytes_accessed=1, transcendentals=0)


def params(mebibytes):
    return pltpu.CompilerParams(vmem_limit_bytes=mebibytes * 1024 * 1024)


def half_rows(place_ref, ref, start, size):
    half = ref.shape[0] // 2
    return ref[pl.ds(pl.multiple_of(place_ref[0] * half, half) + start, size)]


def half_rows_of(place_ref, refs, start, size):
    rows = refs[0].shape[0]
    side = len(refs) // 2
    piece, first = start // rows, start % rows
    span = slice(first, first + size)
    return jnp.where(place_ref[0] == 0, refs[piece][span], refs[side + piece][span])


def cross_products(place_ref, own_ref, next_refs, far_ref, start):
    rows, width = far_ref.shape
    total = jnp.zeros((width, 2 * width), F32)
    for span in tiles(rows):
        first, size = start + span.start, span.stop - span.start
        here = [
            half_rows(place_ref, own_ref, first, size),
            half_rows_of(place_ref, next_refs, first, size),
        ]
        total += product(split(far_ref[span]), split(jnp.concatenate(here, 1)), TN)
    return total


def first_kernel(place_ref, own_ref, far_ref, listed_ref, *rest):
    next_refs, out_ref = rest[:-1], rest[-1]
    rows, width = own_ref.shape
    chunk = rows // len(next_refs)
    total = jnp.zeros((width, 2 * width), F32)
    for number, next_ref in enumerate(next_refs):
        span = slice(number * chunk, (number + 1) * chunk)
        own, neighbour = split(own_ref[span]), split(next_ref[...])
        pair = [jnp.concatenate([a, b], 1) for a, b in zip(own, neighbour)]
        total += product(own, pair, TN)
    cross = cross_products(place_ref, own_ref, next_refs, far_ref, 0)
    for number, part in enumerate([cross, total]):
        out_ref[2 * number * width : (2 * number + 1) * width] = part[:, :width]
        out_ref[(2 * number + 1) * width : (2 * number + 2) * width] = part[:, width:]
    out_ref[4 * width :] = listed_ref[...]


def last_kernel(start, place_ref, own_ref, far_ref, before_ref, *rest):
    next_refs, out_ref = rest[:-1], rest[-1]
    width = own_ref.shape[1]
    cross = cross_products(place_ref, own_ref, next_refs, far_ref, start)
    out_ref[:width] = before_ref[:width] + cross[:, :width]
    out_ref[width : 2 * width] = before_ref[width : 2 * width] + cross[:, width:]
    out_ref[2 * width :] = before_ref[2 * width :]


def gram_call(kernel, name, place, *values):
    width = values[0].shape[1]
    return pl.pallas_call(
        kernel,
        in_specs=[SMEM] + [VMEM] * len(values),
        out_specs=VMEM,
        out_shape=array(4 * width + 8, width),
        compiler_params=params(12),
        cost_estimate=BRIEF,
        name=name,
    )(place, *values)


def rotations(grams, sign):
    width = grams[0].shape[0]
    half = width // 2
    row = lax.broadcasted_iota(jnp.int32, (width, width), 0)
    column = lax.broadcasted_iota(jnp.int32, (width, width), 1)
    diagonal = (row == column).astype(F32)
    order = jnp.where(row < column, 0.5, -0.5) * (1.0 - diagonal)
    order = jnp.where((row < half) == (column < half), order, order * sign)
    iterates = []
    for gram in grams:
        inverse_row = 1.0 / jnp.sqrt(jnp.sum(gram * diagonal, axis=0, keepdims=True))
        inverse_column = 1.0 / jnp.sqrt(jnp.sum(gram * diagonal, axis=1, keepdims=True))
        skew = gram * inverse_column * inverse_row * order
        iterates.append((diagonal + skew) / jnp.sqrt(1.0 + jnp.sum(skew * skew)))
    for step in range(NS_STEPS):
        parts = [split(iterate) for iterate in iterates]
        squares = [product(part, part, NT) for part in parts]
        rests = [0.5 * (diagonal - square) for square in squares]
        iterates = [
            iterate + product(part, split(rest), NN)
            for iterate, part, rest in zip(iterates, parts, rests)
        ]
    return iterates


def symmetric(first, cross, second):
    return jnp.concatenate(
        [jnp.concatenate([first, cross], 1), jnp.concatenate([cross.T, second], 1)], 0
    )


def kept_row(listed):
    width = listed.shape[1]
    row = lax.broadcasted_iota(jnp.int32, (width // 2, width), 0)
    column = lax.broadcasted_iota(jnp.int32, (width // 2, width), 1)
    numbers = jnp.sum(jnp.where(row == column, listed, 0.0), axis=1, keepdims=True)
    return jnp.sum((numbers == column.astype(F32)).astype(F32), axis=0, keepdims=True)


def turn_kernel(place_ref, mine_ref, far_ref, next_ref, next_far_ref, first_ref, second_ref, norm_ref):
    width = mine_ref.shape[1]
    sign_far = jnp.where(place_ref[0] == 0, 1.0, -1.0)
    sign_next = jnp.where(place_ref[1] == 0, 1.0, -1.0)
    refs = (mine_ref, far_ref, next_ref, next_far_ref)
    mine, far, neighbour, next_far = [
        [ref[number * width : (number + 1) * width] for number in range(4)] for ref in refs
    ]
    kept_rows = [kept_row(ref[4 * width : 4 * width + 1]) for ref in refs]
    lo, hi = slice(0, width), slice(width, 2 * width)
    gram_01 = symmetric(mine[2], mine[0].T + far[0], far[2])
    gram_23 = symmetric(neighbour[2], neighbour[0].T + next_far[0], next_far[2])
    gram_03 = far[1] + neighbour[1].T
    gram_12 = mine[1] + next_far[1].T
    mixed = jnp.concatenate(
        [jnp.concatenate([mine[3], gram_03], 1), jnp.concatenate([gram_12, far[3]], 1)], 0
    )
    turn_01, turn_23 = rotations([gram_01, gram_23], sign_far)
    s_01, s_23 = split(turn_01), split(turn_23)
    s_01t, s_23t = split(turn_01.T), split(turn_23.T)
    half_01 = split(product(split(gram_01), s_01, NN))
    half_23 = split(product(split(gram_23), s_23, NN))
    half_mixed = split(product(split(mixed), s_23, NN))

    def corner(left, right, which):
        return product([p[which] for p in left], [p[:, which] for p in right], NN)

    grams = [
        symmetric(corner(s_01t, half_01, w), corner(s_01t, half_mixed, w), corner(s_23t, half_23, w))
        for w in (lo, hi)
    ]
    seconds = rotations(grams, sign_next)

    first_ref[0], first_ref[1] = turn_01, turn_23
    total = jnp.zeros((1, 1), F32)
    for number, (gram, second) in enumerate(zip(grams, seconds)):
        second_ref[number] = second[:, :width]
        moved = product(split(gram), split(second), NN) * second
        kept = jnp.concatenate([kept_rows[number], kept_rows[number + 2]], 1)
        total += jnp.sum(jnp.sum(moved, axis=0, keepdims=True) * kept, axis=1, keepdims=True)
    norm_ref[...] = jnp.broadcast_to(total, norm_ref.shape)


def turn(place, *values):
    width = values[0].shape[1]
    return pl.pallas_call(
        turn_kernel,
        in_specs=[SMEM] + [VMEM] * len(values),
        out_specs=[VMEM] * 3,
        out_shape=[
            array(2, 2 * width, 2 * width),
            array(2, 2 * width, width),
            array(8, width),
        ],
        compiler_params=params(24),
        name="turn",
    )(place, *values)


def route_kernel(first_ref, second_ref, route_ref, high_ref, low_ref):
    width = second_ref.shape[2]
    firsts = [split(first_ref[number]) for number in range(2)]
    totals = [0.0, 0.0]
    for number in range(2):
        second = split(second_ref[number])
        which = slice(number * width, (number + 1) * width)
        turned = jnp.concatenate(
            [
                product(
                    [piece[:, which] for piece in first],
                    [piece[side * width : (side + 1) * width] for piece in second],
                    NN,
                )
                for side, first in enumerate(firsts)
            ],
            0,
        )
        route = route_ref[number].astype(BF16)
        totals = [total + dot(piece, route, NN) for total, piece in zip(totals, split(turned))]
    high_ref[...] = totals[0].astype(BF16)
    low_ref[...] = totals[1].astype(BF16)


def routed(first, second, routes):
    shape = jax.ShapeDtypeStruct((2 * first.shape[1], routes.shape[2]), BF16)
    return pl.pallas_call(
        route_kernel,
        in_specs=[VMEM] * 3,
        out_specs=[VMEM] * 2,
        out_shape=[shape, shape],
        compiler_params=params(12),
        cost_estimate=BRIEF,
        name="routed",
    )(first, second, routes)


def sum_kernel(left_ref, right_ref, *rest):
    rest[-1][...] = left_ref[...] + right_ref[...]


def sum_after(left, right, *first):
    return pl.pallas_call(
        sum_kernel,
        in_specs=[VMEM, VMEM] + [ANY] * len(first),
        out_specs=VMEM,
        out_shape=array(*left.shape),
        compiler_params=params(8),
        cost_estimate=BRIEF,
        name="sum_after",
    )(left, right, *first)


def place_kernel(spans, count, place_ref, high_ref, low_ref, block_ref, *rest):
    next_refs, rest = rest[:count], rest[count:]
    far_refs, next_far_refs, out_ref = rest[: len(spans)], rest[len(spans) : 2 * len(spans)], rest[-1]
    width = block_ref.shape[1]
    top, bottom = [
        [ref[side * 2 * width : (side + 1) * 2 * width] for ref in (high_ref, low_ref)]
        for side in range(2)
    ]
    done = 0
    for far_ref, next_far_ref, (start, span) in zip(far_refs, next_far_refs, spans):
        for tile in tiles(span.stop - span.start):
            size = tile.stop - tile.start
            there = slice(span.start + tile.start, span.start + tile.stop)
            here = [
                half_rows(place_ref, block_ref, start + tile.start, size),
                half_rows_of(place_ref, next_refs, start + tile.start, size),
            ]
            near = split(jnp.concatenate([here[0], far_ref[there]], 1))
            away = split(jnp.concatenate([here[1], next_far_ref[there]], 1))
            out_ref[:, done : done + size] = (product(near, top, NN) + product(away, bottom, NN)).T
            done += size


def placed(place, parts, own, neighbour, far, next_far, spans):
    width = own.shape[1]
    rows = sum(span.stop - span.start for _, span in spans)
    return pl.pallas_call(
        functools.partial(place_kernel, spans, len(neighbour)),
        in_specs=[SMEM] + [VMEM] * (3 + len(neighbour) + 2 * len(far)),
        out_specs=VMEM,
        out_shape=array(parts[0].shape[1], rows),
        compiler_params=params(16),
        cost_estimate=pl.CostEstimate(
            flops=48 * rows * width * width, bytes_accessed=16 * rows * width, transcendentals=0
        ),
        name="placed",
    )(place, *parts, own, *neighbour, *far, *next_far)


def spread_kernel(total, *refs):
    norm_ref, other_ref, out_ref = refs[-3:]
    scale = jnp.sqrt(total / (norm_ref[0:1, 0:1] + other_ref[0:1, 0:1]))
    done = 0
    for ref in refs[:-3]:
        for tile in range(ref.shape[1] // LANES):
            value = ref[:, tile * LANES : (tile + 1) * LANES] * scale
            out_ref[:, done] = value.reshape(out_ref.shape[0], out_ref.shape[2], LANES)
            done += 1


def spread(values, norms, total, capacity):
    count = sum(value.shape[1] for value in values) // LANES
    return pl.pallas_call(
        functools.partial(spread_kernel, total),
        in_specs=[VMEM] * (len(values) + 2),
        out_specs=VMEM,
        out_shape=array(values[0].shape[0] // capacity, count, capacity, LANES),
        compiler_params=params(8),
        name="spread",
    )(*values, *norms)


def join_kernel(tiles_ref, out_ref):
    for tile in range(tiles_ref.shape[1]):
        out_ref[:, :, tile * LANES : (tile + 1) * LANES] = tiles_ref[:, tile]


def join(tiles):
    groups, count, capacity, _ = tiles.shape
    return pl.pallas_call(
        join_kernel,
        in_specs=[VMEM],
        out_specs=VMEM,
        out_shape=array(groups, capacity, count * LANES),
        compiler_params=params(8),
        name="join",
    )(tiles)


def from_partner(value, axis, distance):
    pairs = [(source, source ^ distance) for source in range(lax.axis_size(axis))]
    return lax.ppermute(value, axis, pairs)


def route_of(listed, side, groups):
    width = listed.shape[0]
    kept = width // 2
    keep, owners = listed.astype(jnp.int32).reshape(2, kept)
    order = jnp.arange(kept, dtype=jnp.int32)
    same = owners[:, None] == owners[None, :]
    slot = jnp.sum((same & (order[None, :] < order[:, None])).astype(jnp.int32), axis=1)
    capacity = max(2, 2 * kept // groups)
    target = (owners * 2 + side) * capacity + slot
    places = jnp.arange(2 * groups * capacity, dtype=jnp.int32)
    columns = jnp.arange(width, dtype=jnp.int32)
    picked = (keep[:, None] == columns[None, :]).astype(BF16)
    placed = (target[:, None] == places[None, :]).astype(BF16)
    return lax.dot_general(picked, placed, (TN, ((), ())), preferred_element_type=F32)


def on_device(two_site, keep_list, owner_map):
    block = two_site[0]
    rows, width = block.shape
    half = rows // 2
    count, groups = lax.axis_size("bond"), lax.axis_size("site")
    far = count // 2
    position = lax.axis_index("bond")
    upper = position // far
    place = jnp.stack([upper, position & 1]).astype(jnp.int32)

    sizes = piece_sizes(half)
    starts = [(1 - upper) * half + sum(sizes[:number]) for number in range(len(sizes))]
    listed = jnp.concatenate([keep_list[0], owner_map[0, :, 0]]).astype(F32)
    listed = jnp.broadcast_to(listed, (8, width))
    sources = (block, lax.optimization_barrier(block))
    sent = [
        lax.dynamic_slice_in_dim(source, start, size)
        for source, start, size in zip(sources, starts, sizes)
    ]
    quarter = rows // 4
    neighbour = [
        from_partner(block[number * quarter : (number + 1) * quarter], "bond", 1)
        for number in range(4)
    ]
    far_a, far_b = [from_partner(piece, "bond", far) for piece in sent]
    grams = gram_call(first_kernel, "first_gram", place, block, far_a, listed, *neighbour)
    grams = gram_call(
        functools.partial(last_kernel, sizes[0]),
        "last_gram", place, block, far_b, grams, *neighbour,
    )
    far_grams = from_partner(grams, "bond", far)
    next_grams = [from_partner(value, "bond", 1) for value in (grams, far_grams)]
    next_far_a, next_far_b = [from_partner(value, "bond", 1) for value in (far_a, far_b)]
    routes = jnp.stack(
        [
            route_of(listed[0], upper, groups),
            route_of(far_grams[4 * width], 1 - upper, groups),
        ]
    )

    first, second, squares = turn(place, grams, far_grams, *next_grams)
    parts = routed(first, second, routes)
    squares = sum_after(
        squares, from_partner(squares, "bond", 2), parts[0], next_far_a, next_far_b
    )
    outgoing = placed(
        place, parts, block, neighbour, (far_a, far_b), (next_far_a, next_far_b),
        ((0, slice(0, sizes[0])), (sizes[0], slice(0, sizes[1]))),
    )
    norms = (squares, from_partner(squares, "bond", 4))
    keep_count = keep_list.shape[1]
    capacity = max(2, 2 * keep_count // groups)
    members = [
        [(first + far * side) * groups + site for site in range(groups) for side in range(2)]
        for first in range(far)
    ]
    arrived = lax.all_to_all(
        spread([outgoing], norms, float(rows * count * keep_count), capacity),
        ("bond", "site"),
        split_axis=0,
        concat_axis=0,
        tiled=True,
        axis_index_groups=members,
    )
    joined = join(arrived.reshape(groups, rows // LANES, capacity, LANES))
    return joined.reshape(1, 1, groups, capacity, rows)


def solution(mesh):
    return jax.shard_map(
        on_device,
        mesh=mesh,
        in_specs=(P("site", None, "bond"), P("site", "bond"), P("site", "bond", None)),
        out_specs=P("site", "bond", None, None, None),
        check_vma=False,
    )
```
